32 devices in a mesh: dp: 4 (over y, x), tensor: 8 (over z, core).
Axes of the slice: x: 2, y: 2, z: 4, core: 2. Of those that a mesh axis runs over, the one named last changes fastest.
Arguments:
- tokens: bfloat16 [4096, 2048], P(('dp', 'tensor')), may hold values from -6 to 6
- norm_gain: bfloat16 [2048], replicated, may hold values from 0.099609375 to 1.8984375
- routes: int32 [4096, 6], P(('dp', 'tensor')), may hold values from 0 to 31, all different within a row; in each aligned block of 128 rows (0 to 127, 128 to 255, ...) at most 32 rows name the same one
- route_gates: bfloat16 [4096, 6], P(('dp', 'tensor')), may hold values from 0.19921875 to 1
- lengths: int32 [24], replicated, may hold values from 1 to 480, 4096 in all
- request_adapter: int32 [24], replicated, may hold values from 0 to 31
- adapter_slot: int32 [32], replicated, may hold values from 0 to 31, each once
- expert_gate: bfloat16 [32, 2048, 1408], P('tensor'), may hold values from -0.125 to 0.125
- expert_up: bfloat16 [32, 2048, 1408], P('tensor'), may hold values from -0.125 to 0.125
- expert_down: bfloat16 [32, 1408, 2048], P('tensor'), may hold values from -0.15625 to 0.15625
- shared_gate: bfloat16 [2048, 1408], P(None, 'dp'), may hold values from -0.125 to 0.125
- shared_up_weight: bfloat16 [2048, 1408], P(None, 'dp'), may hold values from -0.125 to 0.125
- shared_down: bfloat16 [1408, 2048], P('dp'), may hold values from -0.15625 to 0.15625
- adapter_down: bfloat16 [32, 2048, 16], P('dp'), may hold values from -0.125 to 0.125
- adapter_up: bfloat16 [32, 16, 2048], P('dp'), may hold values from -1.5 to 1.5
- head_weight: bfloat16 [2048, 65536], P(None, ('dp', 'tensor')), may hold values from -0.375 to 0.375
Outputs:
- sublayer_out: bfloat16 [4096, 2048], P(('dp', 'tensor'))
- last_norm: float32 [24], replicated
- block_logit: float32 [24, 8], P(None, 'tensor')
The draws below stay inside these ranges and needn't reach their ends.
Inputs may be any that keep to these rules, and one draw needn't show every extreme that they name: `routes`: in each aligned block of 128 rows (the rows of one device), no expert is named by more than 32 rows, a bound that some block reaches. The lengths sum to 4096; the largest is exactly 480. Each position of the store appears once: adapter a is stored at position adapter_slot[a] of adapter_down and adapter_up.
All inputs are finite; a program needn't handle non-finite values.
Results may differ from the reference program's by a relative error of at most 0.0066.
Values may be sent and summed in bfloat16 or wider, within the bound.
No kernel may reach another device: no remote copies, remote signals or barrier semaphores. Data moves between devices by JAX's collectives and lax.ppermute only.
A program may use at most 192 MiB of HBM per device.

```python
import math
import jax
import jax.numpy as jnp
import numpy as np
from jax import lax

D = 2048
FF = 1408
SFF = 1408
EXPERTS = 32
TOP = 6
RANK = 16
ADAPTERS = 32
VOCAB = 65536
REQUESTS = 24
TOK_DEV = 128
TOKENS = 4096
CAP = 32
LONGEST_LENGTH = 480
N_DP = 4
N_TENSOR = 8
DEVICES = 32


def set_ends(values, own_key, smallest, largest):
    extent = values.shape
    index_at = [jax.random.randint(jax.random.fold_in(own_key, axis), (), 0, extent[axis]) for axis in range(len(extent))]
    values = values.at[tuple(index_at)].set(smallest)
    longest = extent.index(max(extent))
    index_at[longest] = (index_at[longest] + 1) % extent[longest]
    return values.at[tuple(index_at)].set(largest)


def block_levels(key, shape, split, smallest, top_value):
    def one(axis_at, parts):
        steps = jax.random.uniform(jax.random.fold_in(jax.random.fold_in(key, 6), axis_at), (parts,), jnp.float32, smallest / len(split), top_value / len(split))
        return jnp.repeat(jnp.exp(steps), shape[axis_at] // parts).reshape((-1,) + (1,) * (len(shape) - axis_at - 1))

    gain = one(*split[0])
    for cut in split[1:]:
        gain = gain * one(*cut)
    return gain


def cumulative_ranks(amount, skew):
    loads = [(1 << 20) // math.isqrt(rank ** skew) + 1 for rank in range(1, amount + 1)]
    deviation = 1 + sum(loads) // (1 << 30)
    return np.cumsum(np.array([max(1, weight // deviation) for weight in loads]))


def skewed_ids(stream_key, shape, amount, lean):
    grid = cumulative_ranks(amount, lean)
    pick = jax.random.randint(jax.random.fold_in(stream_key, 1), shape, 0, int(grid[amount - 1]))
    grade = jnp.searchsorted(jnp.asarray(grid, jnp.int32), pick, side="right")
    return jax.random.permutation(jax.random.fold_in(stream_key, 2), amount)[grade].astype(jnp.int32)


def split_up(number_of, total, bound, slope):
    loads = [(1 << 20) // math.isqrt(standing ** slope) + 1 for standing in range(2, number_of + 1)]
    rest, counts = total - bound - (number_of - 1), [1] * (number_of - 1)
    while rest > 0:
        movable = [i for i in range(number_of - 1) if counts[i] < bound]
        whole, remaining = sum([loads[i] for i in movable]), rest
        for i in movable:
            more = min(bound - counts[i], max(1, remaining * loads[i] // whole), rest)
            counts[i] = counts[i] + more
            rest = rest - more
    return np.array([bound] + counts)


def ragged_sizes(rng, amount, total, reach, skew):
    if amount == 2:
        one = jax.random.randint(rng, (), max(1, total - reach), min(reach, total - 1) + 1)
        return jnp.stack([one, total - one])
    sizes = jnp.asarray(split_up(amount, total, reach, skew), jnp.int32)
    twos = (amount - 1) // 2
    giver, taker = sizes[1:1 + 2 * twos:2], sizes[2:2 + 2 * twos:2]
    room = jnp.minimum(giver - 1, reach - taker)
    passed = jax.random.randint(jax.random.fold_in(rng, 1), (twos,), 0, 1 << 20) % (room + 1)
    sizes = sizes.at[1:1 + 2 * twos:2].set(giver - passed).at[2:2 + 2 * twos:2].set(taker + passed)
    return sizes[jax.random.permutation(jax.random.fold_in(rng, 2), amount)]


def deal_out(own_key, own, number, rows, number_of, top, limit, lean):
    sequence = jax.random.permutation(own_key, number_of)
    packed, usual = shares(number_of, rows * top, limit, lean, True), shares(number_of, rows * top, limit, lean, False)
    places = jnp.arange(number_of)

    def named(sizes, rotation):
        used = int((sizes > 0).sum())
        fixed = max(1, used // 4)
        shifted = fixed + (places - fixed + rotation * (used - fixed)) % max(1, number_of - fixed)
        return jnp.zeros((number_of,), jnp.int32).at[sequence[jnp.where(places < fixed, places, shifted)]].set(jnp.asarray(sizes, jnp.int32))

    sizes = jnp.where(number % 4 == 0, named(packed, number // 4), named(usual, number - number // 4 - 1))
    mixed = jax.random.permutation(jax.random.fold_in(own, 3), number_of)
    source_of, sink = mixed[0:number_of // 2 * 2:2], mixed[1:number_of // 2 * 2:2]
    margin = jnp.minimum(sizes[source_of] - 1, limit - sizes[sink]) // 2
    margin = jnp.where((source_of == sequence[0]) | (sink == sequence[0]) | (sizes[sink] == 0), 0, jnp.maximum(margin, 0))
    shifted = jax.random.randint(jax.random.fold_in(own, 4), (number_of // 2,), 0, 1 << 20) % (margin + 1)
    sizes = sizes.at[source_of].add(-shifted).at[sink].add(shifted)
    items = jnp.searchsorted(jnp.cumsum(sizes), jnp.arange(rows * top), side="right").astype(jnp.int32)
    table = items.reshape(top, rows).T
    table = table[jax.random.permutation(jax.random.fold_in(own, 1), rows)]
    rotation = jax.random.randint(jax.random.fold_in(own, 2), (rows, 1), 0, top)
    return jnp.take_along_axis(table, (jnp.arange(top)[None, :] + rotation) % top, axis=1)


def shares(count, total, reach, lean, full):
    weights = [(1 << 20) // math.isqrt(grade ** lean) + 1 for grade in range(1, count + 1)]
    largest = reach if full else min(reach, max(-(-total // count), total * weights[0] // sum(weights)))
    least = 1 if total - largest >= count - 1 else 0
    given, spare = [largest] + [least] * (count - 1), total - largest - least * (count - 1)
    while spare > 0:
        free = [i for i in range(1, count) if given[i] < largest] or [i for i in range(1, count) if given[i] < reach]
        mass, remaining = sum([weights[i] for i in free]), spare
        for i in free:
            addition = min(reach - given[i], max(1, remaining * weights[i] // mass), spare)
            given[i] = given[i] + addition
            spare = spare - addition
    return np.array(given)


def normal_values(key, extent, deviation, most, pieces=(), kind=jnp.bfloat16):
    values = deviation * jax.random.normal(key, extent, jnp.float32)
    if pieces:
        values = values * block_levels(key, extent, pieces, -0.22, 0.18)
    return jnp.clip(values, -most, most).astype(kind)


def setup_inputs(seed: int = 0) -> dict:
    seeds = jax.random.split(jax.random.key(seed), 17)
    tokens = normal_values(seeds[0], (TOKENS, D), 1.0, 6.0, ((0, 32),))
    norm_gain = jnp.clip(1.0 + 0.18 * jax.random.normal(seeds[1], (D,), jnp.float32), 0.099609375, 1.8984375).astype(jnp.bfloat16)
    routes_keys = jax.random.split(jax.random.fold_in(seeds[2], 1), TOKENS // TOK_DEV)
    routes_turns = jax.random.permutation(jax.random.fold_in(seeds[2], 3), TOKENS // TOK_DEV)
    routes = jax.vmap(lambda own, number: deal_out(jax.random.fold_in(seeds[2], 2), own, number, TOK_DEV, EXPERTS, TOP, CAP, 2))(routes_keys, routes_turns).reshape((TOKENS, TOP))
    route_gates = jnp.clip(0.19921875 + 0.80078125 * jax.random.uniform(seeds[3], (TOKENS, TOP), jnp.float32) ** block_levels(seeds[3], (TOKENS, TOP), ((0, 32),), -0.2, 0.2), 0.19921875, 1.0).astype(jnp.bfloat16)
    lengths = ragged_sizes(seeds[4], REQUESTS, TOKENS, LONGEST_LENGTH, 2).astype(jnp.int32)
    request_adapter = set_ends(skewed_ids(seeds[5], (REQUESTS,), ADAPTERS, 2), jax.random.fold_in(seeds[5], 3), 0, ADAPTERS - 1).astype(jnp.int32)
    adapter_slot = jax.random.permutation(seeds[6], ADAPTERS).astype(jnp.int32)
    expert_gate = normal_values(seeds[7], (EXPERTS, D, FF), D ** -0.5, 0.125, ((0, 8),))
    expert_up = normal_values(seeds[8], (EXPERTS, D, FF), D ** -0.5, 0.125, ((0, 8),))
    expert_down = normal_values(seeds[9], (EXPERTS, FF, D), FF ** -0.5, 0.15625, ((0, 8),))
    shared_gate = normal_values(seeds[10], (D, SFF), D ** -0.5, 0.125, ((1, 4),))
    shared_up_weight = normal_values(seeds[11], (D, SFF), D ** -0.5, 0.125, ((1, 4),))
    shared_down = normal_values(seeds[12], (SFF, D), SFF ** -0.5, 0.15625, ((0, 4),))
    adapter_down = normal_values(seeds[13], (ADAPTERS, D, RANK), D ** -0.5, 0.125, ((0, 4),))
    adapter_up = normal_values(seeds[14], (ADAPTERS, RANK, D), RANK ** -0.5, 1.5, ((0, 4),))
    head_weight = normal_values(seeds[15], (D, VOCAB), (D // 9) ** -0.5, 0.375, ((1, 32),))
    return {"tokens": tokens, "norm_gain": norm_gain, "routes": routes, "route_gates": route_gates, "lengths": lengths, "request_adapter": request_adapter, "adapter_slot": adapter_slot, "expert_gate": expert_gate, "expert_up": expert_up, "expert_down": expert_down, "shared_gate": shared_gate, "shared_up_weight": shared_up_weight, "shared_down": shared_down, "adapter_down": adapter_down, "adapter_up": adapter_up, "head_weight": head_weight}


def apply_norm(tokens, norm_gain):
    values = tokens.astype(jnp.float32)
    scaled = lax.rsqrt(lax.optimization_barrier(jnp.mean(values * values, axis=-1, keepdims=True)) + 1e-06)
    return (values * scaled * norm_gain.astype(jnp.float32)).astype(jnp.bfloat16)

def feed_forward(inputs, gate_mat, up_mat, down_mat):
    gate_portion = jnp.dot(inputs, gate_mat, preferred_element_type=jnp.float32)
    up_part = jnp.dot(inputs, up_mat, preferred_element_type=jnp.float32)
    hidden = (jax.nn.silu(gate_portion) * up_part).astype(jnp.bfloat16)
    return jnp.dot(hidden, down_mat, preferred_element_type=jnp.float32)

def token_slots(positions, lengths, request_adapter, adapter_slot):
    request_ends = jnp.cumsum(lengths).astype(jnp.int32)
    request = lax.optimization_barrier(jnp.sum((request_ends[None, :] <= positions[:, None]).astype(jnp.int32), axis=1)).astype(jnp.int32)
    request_pick = request[:, None] == jnp.arange(request_adapter.shape[0], dtype=jnp.int32)[None, :]
    adapter = lax.optimization_barrier(jnp.sum(jnp.where(request_pick, request_adapter[None, :], 0), axis=1)).astype(jnp.int32)
    adapter_pick = adapter[:, None] == jnp.arange(adapter_slot.shape[0], dtype=jnp.int32)[None, :]
    return lax.optimization_barrier(jnp.sum(jnp.where(adapter_pick, adapter_slot[None, :], 0), axis=1)).astype(jnp.int32)

def adapter_delta(inputs, slot_ids, down_store, up_store, first_slot):
    held_count = down_store.shape[0]
    model_width = down_store.shape[1]
    rank_size = down_store.shape[2]
    flat_down = jnp.transpose(down_store, (1, 0, 2)).reshape(model_width, held_count * rank_size)
    low_rank = jnp.dot(inputs, flat_down, preferred_element_type=jnp.float32)
    low_rank = low_rank.reshape(inputs.shape[0], held_count, rank_size)
    keep_mask = slot_ids[:, None] == first_slot + jnp.arange(held_count, dtype=jnp.int32)[None, :]
    low_rank = jnp.where(keep_mask[:, :, None], low_rank, 0.0).astype(jnp.bfloat16)
    low_rank = low_rank.reshape(inputs.shape[0], held_count * rank_size)
    flat_up = up_store.reshape(held_count * rank_size, up_store.shape[2])
    return jnp.dot(low_rank, flat_up, preferred_element_type=jnp.float32)

def reference(tokens, norm_gain, routes, route_gates, lengths, request_adapter, adapter_slot, expert_gate, expert_up, expert_down, shared_gate, shared_up_weight, shared_down, adapter_down, adapter_up, head_weight):
    normed = apply_norm(tokens, norm_gain)
    bucket = DEVICES * CAP
    gate_values = route_gates.astype(jnp.float32)

    def one_expert(routed_output, inputs):
        number, gate_mat, up_mat, down_mat = inputs
        route_hits = routes == number
        chosen = jnp.any(route_hits, axis=1)
        weight = lax.optimization_barrier(jnp.sum(jnp.where(route_hits, gate_values, 0.0), axis=1))
        slot_place = (jnp.cumsum(chosen.astype(jnp.int32)) - 1).astype(jnp.int32)
        target = jnp.where(chosen, slot_place, bucket).astype(jnp.int32)
        row_order = jnp.zeros((bucket,), jnp.int32).at[target].set(jnp.arange(TOKENS, dtype=jnp.int32), mode='drop')
        outputs = feed_forward(normed[row_order], gate_mat, up_mat, down_mat).astype(jnp.bfloat16)
        fetched = outputs[jnp.clip(slot_place, 0, bucket - 1)].astype(jnp.float32)
        return (routed_output + weight[:, None] * fetched, None)
    routed_output, ignored = lax.scan(one_expert, jnp.zeros((TOKENS, D), jnp.float32), (jnp.arange(EXPERTS, dtype=jnp.int32), expert_gate, expert_up, expert_down))
    shared_sum = feed_forward(normed, shared_gate, shared_up_weight, shared_down)
    slot_ids = token_slots(jnp.arange(TOKENS, dtype=jnp.int32), lengths, request_adapter, adapter_slot)
    delta = adapter_delta(normed, slot_ids, adapter_down, adapter_up, 0)
    summed = routed_output + shared_sum + delta
    sublayer_out = summed.astype(jnp.bfloat16)
    request_ends = jnp.cumsum(lengths).astype(jnp.int32)
    last_rows = sublayer_out[request_ends - 1]
    last_values = last_rows.astype(jnp.float32)
    last_norm = jnp.sqrt(lax.optimization_barrier(jnp.sum(last_values * last_values, axis=1)))
    logits = jnp.dot(last_rows, head_weight, preferred_element_type=jnp.float32)
    block_logit = lax.optimization_barrier(jnp.max(logits.reshape(REQUESTS, N_DP, N_TENSOR, VOCAB // DEVICES), axis=(1, 3)))
    return (sublayer_out, last_norm, block_logit)
```

```python
import functools

import jax
import jax.numpy as jnp
from jax import lax
from jax.experimental import pallas as pl
from jax.experimental.pallas import tpu as pltpu
from jax.sharding import PartitionSpec as P

CAP = 32


def apply_norm(tokens, norm_gain):
    values = tokens.astype(jnp.float32)
    scaled = lax.rsqrt(jnp.mean(values * values, axis=-1, keepdims=True) + 1e-06)
    return (values * scaled * norm_gain.astype(jnp.float32)).astype(jnp.bfloat16)


def feed_forward(inputs, gate_mat, up_mat, down_mat):
    gate_portion = jnp.dot(inputs, gate_mat, preferred_element_type=jnp.float32)
    up_part = jnp.dot(inputs, up_mat, preferred_element_type=jnp.float32)
    hidden = (jax.nn.silu(gate_portion) * up_part).astype(jnp.bfloat16)
    return jnp.dot(hidden, down_mat, preferred_element_type=jnp.float32)


def token_slots(positions, lengths, request_adapter, adapter_slot):
    request_ends = jnp.cumsum(lengths)
    request = jnp.sum((request_ends[None, :] <= positions[:, None]).astype(jnp.int32), axis=1)
    request_pick = (
        request[:, None] == jnp.arange(request_adapter.shape[0], dtype=jnp.int32)[None, :]
    )
    adapter = jnp.sum(jnp.where(request_pick, request_adapter[None, :], 0), axis=1)
    adapter_pick = adapter[:, None] == jnp.arange(adapter_slot.shape[0], dtype=jnp.int32)[None, :]
    return jnp.sum(jnp.where(adapter_pick, adapter_slot[None, :], 0), axis=1)


def adapter_delta(inputs, slot_ids, down_store, up_store):
    held_count = down_store.shape[0]
    model_width = down_store.shape[1]
    rank_size = down_store.shape[2]
    flat_down = jnp.transpose(down_store, (1, 0, 2)).reshape(model_width, held_count * rank_size)
    low_rank = jnp.dot(inputs, flat_down, preferred_element_type=jnp.float32)
    low_rank = low_rank.reshape(inputs.shape[0], held_count, rank_size)
    keep_mask = slot_ids[:, None] == jnp.arange(held_count, dtype=jnp.int32)[None, :]
    low_rank = jnp.where(keep_mask[:, :, None], low_rank, 0.0).astype(jnp.bfloat16)
    low_rank = low_rank.reshape(inputs.shape[0], held_count * rank_size)
    flat_up = up_store.reshape(held_count * rank_size, up_store.shape[2])
    return jnp.dot(low_rank, flat_up, preferred_element_type=jnp.float32)


def local(
    tokens,
    norm_gain,
    routes,
    route_gates,
    lengths,
    request_adapter,
    adapter_slot,
    expert_gate,
    expert_up,
    expert_down,
    shared_gate,
    shared_up_weight,
    shared_down,
    adapter_down,
    adapter_up,
    head_weight,
):
    tok_rows = tokens.shape[0]
    model_width = tokens.shape[1]
    route_count = routes.shape[1]
    tensor_size = lax.axis_size("tensor")
    tensor_pos = lax.axis_index("tensor")
    data_pos = lax.axis_index("dp")
    local_experts = expert_gate.shape[0]
    all_experts = local_experts * tensor_size
    slot_range = jnp.arange(CAP, dtype=jnp.int32)
    normed = apply_norm(tokens, norm_gain)
    numbers = jnp.arange(all_experts, dtype=jnp.int32)
    route_hits = routes[:, :, None] == numbers[None, None, :]
    chosen = jnp.any(route_hits, axis=1)
    weight = jnp.sum(
        jnp.where(route_hits, route_gates[:, :, None], jnp.zeros((), jnp.bfloat16)), axis=1
    )
    slot_place = jnp.cumsum(chosen.astype(jnp.int32), axis=0) - 1
    pooled, pooled_routes = (
        lax.all_gather(normed, "tensor", axis=0, tiled=True),
        lax.all_gather(routes.astype(jnp.bfloat16), "tensor", axis=0, tiled=True),
    )
    pooled = pooled.reshape(tensor_size, tok_rows, model_width)
    source_routes = pooled_routes.astype(jnp.int32).reshape(tensor_size, tok_rows, route_count)
    own_numbers = tensor_pos * local_experts + jnp.arange(local_experts, dtype=jnp.int32)
    source_hits = source_routes[:, :, :, None] == own_numbers[None, None, None, :]
    source_chosen = jnp.any(source_hits, axis=2)
    source_place = jnp.cumsum(source_chosen.astype(jnp.int32), axis=1) - 1
    source_pick = source_chosen[:, :, :, None] & (
        source_place[:, :, :, None] == slot_range[None, None, None, :]
    )
    source_pick = jnp.where(source_pick, 1.0, 0.0).astype(jnp.bfloat16)
    incoming = jnp.einsum(
        "sijc,sid->sjcd", source_pick, pooled, preferred_element_type=jnp.float32
    ).astype(jnp.bfloat16)
    gate_portion = jnp.einsum(
        "secd,edf->secf", incoming, expert_gate, preferred_element_type=jnp.float32
    )
    up_part = jnp.einsum("secd,edf->secf", incoming, expert_up, preferred_element_type=jnp.float32)
    hidden = (jax.nn.silu(gate_portion) * up_part).astype(jnp.bfloat16)
    expert_out = jnp.einsum(
        "secf,efd->secd", hidden, expert_down, preferred_element_type=jnp.float32
    ).astype(jnp.bfloat16)
    returned_rows = lax.all_to_all(expert_out, "tensor", split_axis=0, concat_axis=0, tiled=True)
    returned_rows = returned_rows.reshape(all_experts, CAP, model_width)
    mixing_result = jnp.where(
        slot_place[:, :, None] == slot_range[None, None, :],
        weight[:, :, None],
        jnp.zeros((), jnp.bfloat16),
    )
    routed_output = jnp.einsum(
        "kbt,btw->kw", mixing_result, returned_rows, preferred_element_type=jnp.float32
    )
    own_base = (data_pos * tensor_size + tensor_pos) * tok_rows
    own_positions = own_base + jnp.arange(tok_rows, dtype=jnp.int32)
    peer_rows = lax.all_gather(normed, "dp", axis=0, tiled=True)
    shared_sum = lax.psum_scatter(
        feed_forward(peer_rows, shared_gate, shared_up_weight, shared_down),
        "dp",
        scatter_dimension=0,
        tiled=True,
    )
    own_slots = token_slots(own_positions, lengths, request_adapter, adapter_slot)
    store_down, store_up = (
        lax.all_gather(adapter_down, "dp", axis=0, tiled=True),
        lax.all_gather(adapter_up, "dp", axis=0, tiled=True),
    )
    summed = routed_output + shared_sum + adapter_delta(normed, own_slots, store_down, store_up)
    sublayer_out = summed.astype(jnp.bfloat16)
    request_ends = jnp.cumsum(lengths)
    last_pick = jnp.where(request_ends[:, None] - 1 == own_positions[None, :], 1.0, 0.0).astype(
        jnp.bfloat16
    )
    last_part = jnp.dot(last_pick, sublayer_out, preferred_element_type=jnp.float32)
    last_states = lax.psum(last_part, ("dp", "tensor"))
    last_norm = jnp.sqrt(jnp.sum(last_states * last_states, axis=1))
    logits = jnp.dot(
        last_states.astype(jnp.bfloat16), head_weight, preferred_element_type=jnp.float32
    )
    block_logit = lax.pmax(jnp.max(logits, axis=1), "dp")
    return (sublayer_out, last_norm, block_logit[:, None])


def prep_kernel(tok_ref, gain_ref, routes_ref, gates_ref, first_ref, second_ref, whole_ref):
    rows = tok_ref.shape[0]
    half = second_ref.shape[1]
    experts = 32
    values = tok_ref[...].astype(jnp.float32)
    scaled = lax.rsqrt(jnp.mean(values * values, axis=-1, keepdims=True) + 1e-06)
    normed = (values * scaled * gain_ref[...].astype(jnp.float32)).astype(jnp.bfloat16)
    whole_ref[...] = normed
    first_ref[:, :half] = normed[:, :half]
    second_ref[...] = normed[:, half:]
    numbers = lax.broadcasted_iota(jnp.int32, (rows, experts), 1)
    chosen = jnp.zeros((rows, experts), jnp.float32)
    weight = jnp.zeros((rows, experts), jnp.float32)
    for k in range(routes_ref.shape[1]):
        hit = routes_ref[:, k : k + 1] == numbers
        chosen = jnp.where(hit, 1.0, chosen)
        weight = jnp.where(hit, gates_ref[:, k : k + 1].astype(jnp.float32), weight)
    row = lax.broadcasted_iota(jnp.int32, (rows, rows), 0)
    column = lax.broadcasted_iota(jnp.int32, (rows, rows), 1)
    upto = jnp.where(row <= column, 1.0, 0.0).astype(jnp.bfloat16)
    same = jnp.where(row == column, 1.0, 0.0).astype(jnp.bfloat16)
    turn = (((0,), (0,)), ((), ()))
    chosen = chosen.astype(jnp.bfloat16)
    count = lax.dot_general(chosen, upto, turn, preferred_element_type=jnp.float32)
    taken = lax.dot_general(chosen, same, turn, preferred_element_type=jnp.float32)
    weight = lax.dot_general(
        weight.astype(jnp.bfloat16), same, turn, preferred_element_type=jnp.float32
    )
    place = jnp.where(taken > 0.5, count - 1.0, -1.0)
    first_ref[:experts, half:] = place.astype(jnp.bfloat16)
    first_ref[experts : 2 * experts, half:] = weight.astype(jnp.bfloat16)
    first_ref[2 * experts :, half:] = jnp.zeros((rows - 2 * experts, rows), jnp.bfloat16)


def prepare(tokens, norm_gain, routes, route_gates):
    rows, width = tokens.shape
    half = width // 2
    return pl.pallas_call(
        prep_kernel,
        out_shape=(
            jax.ShapeDtypeStruct((rows, half + rows), jnp.bfloat16),
            jax.ShapeDtypeStruct((rows, half), jnp.bfloat16),
            jax.ShapeDtypeStruct((rows, width), jnp.bfloat16),
        ),
        name="prepare",
    )(tokens, norm_gain.reshape(1, width), routes, route_gates)


def fill_incoming(blocks, places_ref, incoming, width):
    count = (len(blocks) + 1) // 2
    experts = places_ref.shape[1]
    slots = lax.broadcasted_iota(jnp.int32, (CAP, 128), 0)
    for d in range(count):
        for c in range(2):
            picks = [
                jnp.where(places_ref[2 * d + c, e : e + 1, :] == slots, 1.0, 0.0)
                for e in range(experts)
            ]
            pick = jnp.concatenate(picks, axis=0).astype(jnp.bfloat16)
            part = pl.ds(c * 128, 128)
            rows = blocks[d][part, :width]
            if d > 0:
                rows = rows + blocks[2 * count - 1 - d][part, :width]
            chosen = jnp.dot(pick, rows, preferred_element_type=jnp.float32).astype(jnp.bfloat16)
            for e in range(experts):
                at = pl.ds((2 * d + c) * CAP, CAP)
                incoming[e, at, :] = chosen[e * CAP : (e + 1) * CAP]


def first_kernel(places_ref, *refs):
    blocks, (gate_ref, up_ref, gate_out, up_out, incoming) = refs[:-5], refs[-5:]
    e = pl.program_id(0)

    @pl.when(e == 0)
    def _():
        fill_incoming(blocks, places_ref, incoming, incoming.shape[2])

    rows = incoming[e]
    gate_out[0] = jnp.dot(rows, gate_ref[0], preferred_element_type=jnp.float32)
    up_out[0] = jnp.dot(rows, up_ref[0], preferred_element_type=jnp.float32)


def first_half(places, blocks, gate, up):
    sources, experts, _ = places.shape
    half = gate.shape[1] // 2
    hidden = gate.shape[2]
    weight_spec = pl.BlockSpec((1, half, hidden), lambda e: (e, 0, 0))
    out_spec = pl.BlockSpec((1, sources * CAP, hidden), lambda e: (e, 0, 0))
    out_shape = jax.ShapeDtypeStruct((experts, sources * CAP, hidden), jnp.float32)
    whole = lambda a: pl.BlockSpec(a.shape, lambda e: (0,) * a.ndim)
    return pl.pallas_call(
        first_kernel,
        grid=(experts,),
        in_specs=[whole(places)] + [whole(b) for b in blocks] + [weight_spec, weight_spec],
        out_specs=(out_spec, out_spec),
        out_shape=(out_shape, out_shape),
        scratch_shapes=[pltpu.VMEM((experts, sources * CAP, half), jnp.bfloat16)],
        compiler_params=pltpu.CompilerParams(vmem_limit_bytes=48 << 20),
        cost_estimate=pl.CostEstimate(
            flops=4 * experts * sources * CAP * half * hidden,
            bytes_accessed=4 * experts * half * hidden + 8 * experts * sources * CAP * hidden,
            transcendentals=0,
        ),
        name="first_half",
    )(places, *blocks, gate, up)


def second_kernel(experts, places_ref, weights_ref, *refs):
    blocks, rest = refs[:-11], refs[-11:]
    gate_ref, up_ref, gate_acc, up_acc, down_ref, left_ref, right_ref = rest[:7]
    incoming, hidden, outs, mix = rest[7:]
    sources = places_ref.shape[0]
    i = pl.program_id(0)

    @pl.when(i == 0)
    def _():
        fill_incoming(blocks, places_ref, incoming, incoming.shape[2])
        slots = lax.broadcasted_iota(jnp.int32, (CAP, 128), 0)
        for s in range(sources):
            for e in range(experts):
                mix[s, e * CAP : (e + 1) * CAP, :] = jnp.where(
                    places_ref[s, e : e + 1, :] == slots, weights_ref[s, e : e + 1, :], 0.0
                ).astype(jnp.bfloat16)

    @pl.when(i < experts)
    def _():
        rows = incoming[i]
        gate = gate_acc[0] + jnp.dot(rows, gate_ref[0], preferred_element_type=jnp.float32)
        up = up_acc[0] + jnp.dot(rows, up_ref[0], preferred_element_type=jnp.float32)
        hidden[i] = (gate / (1.0 + jnp.exp(-gate)) * up).astype(jnp.bfloat16)

    @pl.when(i >= experts)
    def _():
        step = i - experts
        e = lax.rem(step, experts)
        n = lax.div(step, experts)
        out = jnp.dot(hidden[e], down_ref[0], preferred_element_type=jnp.float32)
        out = out.astype(jnp.bfloat16)
        at = pl.ds(pl.multiple_of(e * CAP, CAP), CAP)
        for s in range(sources):
            outs[s, at, :] = out[s * CAP : (s + 1) * CAP]

        def combine(to_ref):
            for s in range(sources):
                to_ref[s] = lax.dot_general(
                    mix[s], outs[s], (((0,), (0,)), ((), ())), preferred_element_type=jnp.float32
                ).astype(jnp.bfloat16)

        pl.when((e == experts - 1) & (n < 2))(lambda: combine(left_ref))
        pl.when((e == experts - 1) & (n >= 2))(lambda: combine(right_ref))


def second_half(places, weights, blocks, gate, up, gate_acc, up_acc, down):
    sources, experts, rows = places.shape
    half = gate.shape[1] // 2
    width = gate.shape[1]
    hidden = gate.shape[2]
    tile = half // 2
    slots = sources * CAP
    now = lambda i: jnp.minimum(i, experts - 1)
    later = lambda i: jnp.maximum(i - experts, 0)
    weight_spec = pl.BlockSpec((1, half, hidden), lambda i: (now(i), 1, 0))
    acc_spec = pl.BlockSpec((1, slots, hidden), lambda i: (now(i), 0, 0))
    down_spec = pl.BlockSpec(
        (1, hidden, tile), lambda i: (lax.rem(later(i), experts), 0, lax.div(later(i), experts))
    )
    left_spec = pl.BlockSpec(
        (sources, rows, tile), lambda i: (0, 0, jnp.minimum(lax.div(later(i), experts), 1))
    )
    right_spec = pl.BlockSpec(
        (sources, rows, tile), lambda i: (0, 0, jnp.maximum(lax.div(later(i), experts) - 2, 0))
    )
    out_shape = jax.ShapeDtypeStruct((sources, rows, half), jnp.bfloat16)
    whole = lambda a: pl.BlockSpec(a.shape, lambda i: (0,) * a.ndim)
    return pl.pallas_call(
        functools.partial(second_kernel, experts),
        grid=(experts + (width // tile) * experts,),
        in_specs=[whole(places), whole(weights)]
        + [whole(b) for b in blocks]
        + [weight_spec, weight_spec, acc_spec, acc_spec, down_spec],
        out_specs=(left_spec, right_spec),
        out_shape=(out_shape, out_shape),
        scratch_shapes=[
            pltpu.VMEM((experts, slots, half), jnp.bfloat16),
            pltpu.VMEM((experts, slots, hidden), jnp.bfloat16),
            pltpu.VMEM((sources, experts * CAP, tile), jnp.bfloat16),
            pltpu.VMEM((sources, experts * CAP, rows), jnp.bfloat16),
        ],
        compiler_params=pltpu.CompilerParams(vmem_limit_bytes=52 << 20),
        cost_estimate=pl.CostEstimate(
            flops=8 * experts * slots * half * hidden,
            bytes_accessed=8 * experts * half * hidden + 8 * experts * slots * hidden,
            transcendentals=experts * slots * hidden,
        ),
        name="second_half",
    )(places, weights, *blocks, gate, up, gate_acc, up_acc, down)


def add(*terms):
    total = terms[0].astype(jnp.float32)
    for term in terms[1:]:
        total = total + term.astype(jnp.float32)
    return total.astype(jnp.bfloat16)


def swap_cores(value, tensor_size):
    return lax.ppermute(value, "tensor", [(i, i ^ 1) for i in range(tensor_size)])


def spread_pairs(chips, k):
    upward = [(2 * z, 2 * z + 2) for z in range(k - 1, chips - 1)]
    return upward + [(2 * z + 1, 2 * z - 1) for z in range(1, chips - k + 1)]


def collect_pairs(chips, k):
    upward = [(2 * z, 2 * z + 2) for z in range(0, k)]
    return upward + [(2 * z + 1, 2 * z - 1) for z in range(chips - k, chips)]


def spread(chunks, core, tensor_size):
    chips = tensor_size // 2
    last, mine, other = [], [], []
    for chunk in chunks:
        twin = swap_cores(chunk, tensor_size)
        pair = jnp.where(
            core == 0, jnp.concatenate([chunk, twin]), jnp.concatenate([twin, chunk])
        )
        last.append(pair)
        mine.append([pair])
        other.append([])
    for k in range(1, chips):
        for j in range(len(chunks)):
            last[j] = lax.ppermute(last[j], "tensor", spread_pairs(chips, k))
            mine[j].append(last[j])
            other[j].append(swap_cores(last[j], tensor_size))
    return [m + o for m, o in zip(mine, other)]


def collect(parts, core, tensor_size):
    chips = tensor_size // 2
    run = [None] * len(parts)
    for k in range(1, chips):
        for j, part in enumerate(parts):
            got = swap_cores(part[chips - k], tensor_size)
            terms = (part[k], got) if run[j] is None else (part[k], got, run[j])
            run[j] = lax.ppermute(add(*terms), "tensor", collect_pairs(chips, k))
    done = []
    for j, part in enumerate(parts):
        total = add(part[0], run[j])
        rows = total.shape[0] // 2
        low, high = total[:rows], total[rows:]
        got = swap_cores(jnp.where(core == 0, high, low), tensor_size)
        done.append(jnp.where(core == 0, low, high).astype(jnp.float32) + got.astype(jnp.float32))
    return done


def across(value, combine, axis, size):
    step = 1
    while step < size:
        pairs = [(i, i ^ step) for i in range(size)]
        value = combine(value, lax.ppermute(value, axis, pairs))
        step *= 2
    return value


def local_line(
    tokens,
    norm_gain,
    routes,
    route_gates,
    lengths,
    request_adapter,
    adapter_slot,
    expert_gate,
    expert_up,
    expert_down,
    shared_gate,
    shared_up_weight,
    shared_down,
    adapter_down,
    adapter_up,
    head_weight,
):
    tok_rows, width = tokens.shape
    half = width // 2
    tensor_size = lax.axis_size("tensor")
    data_size = lax.axis_size("dp")
    tensor_pos = lax.axis_index("tensor")
    data_pos = lax.axis_index("dp")
    chips = tensor_size // 2
    chip, core = tensor_pos // 2, tensor_pos % 2
    experts = expert_gate.shape[0]
    all_experts = experts * tensor_size
    first, second, normed = prepare(tokens, norm_gain, routes, route_gates)
    blocks_a, blocks_b = spread([first, second], core, tensor_size)
    own_first = tensor_pos * experts

    def held(begin):
        rows = []
        for d in range(chips):
            for c in range(2):
                take = lambda b: lax.dynamic_slice(
                    b[:, half:], (c * tok_rows + begin + own_first, 0), (experts, tok_rows)
                )
                row = take(blocks_a[d])
                if d > 0:
                    row = row + take(blocks_a[2 * chips - 1 - d])
                rows.append(row)
        return jnp.stack(rows)

    places = held(0).astype(jnp.int32)
    weights = held(all_experts).astype(jnp.float32)
    gate_acc, up_acc = first_half(places, blocks_a, expert_gate, expert_up)
    left, right = second_half(
        places, weights, blocks_b, expert_gate, expert_up, gate_acc, up_acc, expert_down
    )
    peer_rows = lax.all_gather(normed, "dp", axis=0, tiled=True)
    block_rows = jnp.arange(tok_rows, dtype=jnp.int32)
    bases = (jnp.arange(data_size, dtype=jnp.int32) * tensor_size + tensor_pos) * tok_rows
    peer_positions = (bases[:, None] + block_rows[None, :]).reshape(-1)
    peer_slots = token_slots(peer_positions, lengths, request_adapter, adapter_slot)
    held_slots = peer_slots - data_pos * adapter_down.shape[0]
    peer_part = feed_forward(peer_rows, shared_gate, shared_up_weight, shared_down)
    peer_part = peer_part + adapter_delta(peer_rows, held_slots, adapter_down, adapter_up)
    peer_part = peer_part.astype(jnp.bfloat16)
    shared_sum = lax.psum_scatter(peer_part, "dp", scatter_dimension=0, tiled=True)
    ends = jnp.cumsum(lengths) - 1
    owner, row = ends // tok_rows, ends % tok_rows
    owner_dp, owner_tensor = owner // tensor_size, owner % tensor_size
    away = jnp.where(core == 0, chip - owner_tensor // 2, owner_tensor // 2 - chip) % chips
    line_row = jnp.where(
        owner_dp == data_pos, (away * 2 + owner_tensor % 2) * tok_rows + row, -1
    )
    peer_row = jnp.where(owner_tensor == tensor_pos, owner_dp * tok_rows + row, -1)

    def pick(at, count):
        return jnp.where(
            at[:, None] == jnp.arange(count, dtype=jnp.int32)[None, :], 1.0, 0.0
        ).astype(jnp.bfloat16)

    line_pick = pick(line_row, 2 * chips * tok_rows)
    last_part = jnp.concatenate(
        [
            jnp.dot(line_pick, p.reshape(-1, half), preferred_element_type=jnp.float32)
            for p in (left, right)
        ],
        axis=1,
    )
    last_part = last_part + jnp.dot(
        pick(peer_row, data_size * tok_rows), peer_part, preferred_element_type=jnp.float32
    )
    last = across(last_part, jnp.add, "tensor", tensor_size)
    last = across(last, jnp.add, "dp", data_size).astype(jnp.bfloat16)
    last_values = last.astype(jnp.float32)
    last_norm = jnp.sqrt(jnp.sum(last_values * last_values, axis=1))
    logits = jnp.dot(last, head_weight, preferred_element_type=jnp.float32)
    block_logit = across(jnp.max(logits, axis=1, keepdims=True), jnp.maximum, "dp", data_size)
    parts = [
        [p.reshape(chips, 2 * tok_rows, half)[d] for d in range(chips)] for p in (left, right)
    ]
    routed = collect(parts, core, tensor_size)
    out = jnp.concatenate(routed, axis=1) + shared_sum.astype(jnp.float32)
    return (out.astype(jnp.bfloat16), last_norm, block_logit)


def solution(mesh):
    placed = (
        P(("dp", "tensor"), None),
        P(),
        P(("dp", "tensor"), None),
        P(("dp", "tensor"), None),
        P(),
        P(),
        P(),
        P("tensor", None, None),
        P("tensor", None, None),
        P("tensor", None, None),
        P(None, "dp"),
        P(None, "dp"),
        P("dp", None),
        P("dp", None, None),
        P("dp", None, None),
        P(None, ("dp", "tensor")),
    )
    short = mesh.shape["tensor"] == 8 and mesh.shape["dp"] == 4
    return jax.shard_map(
        local_line if short else local,
        mesh=mesh,
        in_specs=placed,
        out_specs=(P(("dp", "tensor"), None), P(), P(None, "tensor")),
        check_vma=False,
    )
```

```python
import functools

import jax
import jax.numpy as jnp
from jax import lax
from jax.experimental import pallas as pl
from jax.experimental.pallas import tpu as pltpu
from jax.sharding import PartitionSpec as P

CAP = 32


def apply_norm(tokens, norm_gain):
    values = tokens.astype(jnp.float32)
    scaled = lax.rsqrt(jnp.mean(values * values, axis=-1, keepdims=True) + 1e-06)
    return (values * scaled * norm_gain.astype(jnp.float32)).astype(jnp.bfloat16)


def feed_forward(inputs, gate_mat, up_mat, down_mat):
    gate_portion = jnp.dot(inputs, gate_mat, preferred_element_type=jnp.float32)
    up_part = jnp.dot(inputs, up_mat, preferred_element_type=jnp.float32)
    hidden = (jax.nn.silu(gate_portion) * up_part).astype(jnp.bfloat16)
    return jnp.dot(hidden, down_mat, preferred_element_type=jnp.float32)


def token_slots(positions, lengths, request_adapter, adapter_slot):
    request_ends = jnp.cumsum(lengths)
    request = jnp.sum((request_ends[None, :] <= positions[:, None]).astype(jnp.int32), axis=1)
    request_pick = (
        request[:, None] == jnp.arange(request_adapter.shape[0], dtype=jnp.int32)[None, :]
    )
    adapter = jnp.sum(jnp.where(request_pick, request_adapter[None, :], 0), axis=1)
    adapter_pick = adapter[:, None] == jnp.arange(adapter_slot.shape[0], dtype=jnp.int32)[None, :]
    return jnp.sum(jnp.where(adapter_pick, adapter_slot[None, :], 0), axis=1)


def adapter_delta(inputs, slot_ids, down_store, up_store):
    held_count = down_store.shape[0]
    model_width = down_store.shape[1]
    rank_size = down_store.shape[2]
    flat_down = jnp.transpose(down_store, (1, 0, 2)).reshape(model_width, held_count * rank_size)
    low_rank = jnp.dot(inputs, flat_down, preferred_element_type=jnp.float32)
    low_rank = low_rank.reshape(inputs.shape[0], held_count, rank_size)
    keep_mask = slot_ids[:, None] == jnp.arange(held_count, dtype=jnp.int32)[None, :]
    low_rank = jnp.where(keep_mask[:, :, None], low_rank, 0.0).astype(jnp.bfloat16)
    low_rank = low_rank.reshape(inputs.shape[0], held_count * rank_size)
    flat_up = up_store.reshape(held_count * rank_size, up_store.shape[2])
    return jnp.dot(low_rank, flat_up, preferred_element_type=jnp.float32)


def local(
    tokens,
    norm_gain,
    routes,
    route_gates,
    lengths,
    request_adapter,
    adapter_slot,
    expert_gate,
    expert_up,
    expert_down,
    shared_gate,
    shared_up_weight,
    shared_down,
    adapter_down,
    adapter_up,
    head_weight,
):
    tok_rows = tokens.shape[0]
    model_width = tokens.shape[1]
    route_count = routes.shape[1]
    tensor_size = lax.axis_size("tensor")
    tensor_pos = lax.axis_index("tensor")
    data_pos = lax.axis_index("dp")
    local_experts = expert_gate.shape[0]
    all_experts = local_experts * tensor_size
    slot_range = jnp.arange(CAP, dtype=jnp.int32)
    normed = apply_norm(tokens, norm_gain)
    numbers = jnp.arange(all_experts, dtype=jnp.int32)
    route_hits = routes[:, :, None] == numbers[None, None, :]
    chosen = jnp.any(route_hits, axis=1)
    weight = jnp.sum(
        jnp.where(route_hits, route_gates[:, :, None], jnp.zeros((), jnp.bfloat16)), axis=1
    )
    slot_place = jnp.cumsum(chosen.astype(jnp.int32), axis=0) - 1
    pooled, pooled_routes = (
        lax.all_gather(normed, "tensor", axis=0, tiled=True),
        lax.all_gather(routes.astype(jnp.bfloat16), "tensor", axis=0, tiled=True),
    )
    pooled = pooled.reshape(tensor_size, tok_rows, model_width)
    source_routes = pooled_routes.astype(jnp.int32).reshape(tensor_size, tok_rows, route_count)
    own_numbers = tensor_pos * local_experts + jnp.arange(local_experts, dtype=jnp.int32)
    source_hits = source_routes[:, :, :, None] == own_numbers[None, None, None, :]
    source_chosen = jnp.any(source_hits, axis=2)
    source_place = jnp.cumsum(source_chosen.astype(jnp.int32), axis=1) - 1
    source_pick = source_chosen[:, :, :, None] & (
        source_place[:, :, :, None] == slot_range[None, None, None, :]
    )
    source_pick = jnp.where(source_pick, 1.0, 0.0).astype(jnp.bfloat16)
    incoming = jnp.einsum(
        "sijc,sid->sjcd", source_pick, pooled, preferred_element_type=jnp.float32
    ).astype(jnp.bfloat16)
    gate_portion = jnp.einsum(
        "secd,edf->secf", incoming, expert_gate, preferred_element_type=jnp.float32
    )
    up_part = jnp.einsum("secd,edf->secf", incoming, expert_up, preferred_element_type=jnp.float32)
    hidden = (jax.nn.silu(gate_portion) * up_part).astype(jnp.bfloat16)
    expert_out = jnp.einsum(
        "secf,efd->secd", hidden, expert_down, preferred_element_type=jnp.float32
    ).astype(jnp.bfloat16)
    returned_rows = lax.all_to_all(expert_out, "tensor", split_axis=0, concat_axis=0, tiled=True)
    returned_rows = returned_rows.reshape(all_experts, CAP, model_width)
    mixing_result = jnp.where(
        slot_place[:, :, None] == slot_range[None, None, :],
        weight[:, :, None],
        jnp.zeros((), jnp.bfloat16),
    )
    routed_output = jnp.einsum(
        "kbt,btw->kw", mixing_result, returned_rows, preferred_element_type=jnp.float32
    )
    own_base = (data_pos * tensor_size + tensor_pos) * tok_rows
    own_positions = own_base + jnp.arange(tok_rows, dtype=jnp.int32)
    peer_rows = lax.all_gather(normed, "dp", axis=0, tiled=True)
    shared_sum = lax.psum_scatter(
        feed_forward(peer_rows, shared_gate, shared_up_weight, shared_down),
        "dp",
        scatter_dimension=0,
        tiled=True,
    )
    own_slots = token_slots(own_positions, lengths, request_adapter, adapter_slot)
    store_down, store_up = (
        lax.all_gather(adapter_down, "dp", axis=0, tiled=True),
        lax.all_gather(adapter_up, "dp", axis=0, tiled=True),
    )
    summed = routed_output + shared_sum + adapter_delta(normed, own_slots, store_down, store_up)
    sublayer_out = summed.astype(jnp.bfloat16)
    request_ends = jnp.cumsum(lengths)
    last_pick = jnp.where(request_ends[:, None] - 1 == own_positions[None, :], 1.0, 0.0).astype(
        jnp.bfloat16
    )
    last_part = jnp.dot(last_pick, sublayer_out, preferred_element_type=jnp.float32)
    last_states = lax.psum(last_part, ("dp", "tensor"))
    last_norm = jnp.sqrt(jnp.sum(last_states * last_states, axis=1))
    logits = jnp.dot(
        last_states.astype(jnp.bfloat16), head_weight, preferred_element_type=jnp.float32
    )
    block_logit = lax.pmax(jnp.max(logits, axis=1), "dp")
    return (sublayer_out, last_norm, block_logit[:, None])


AHEAD = 3


def prep_kernel(tok_ref, gain_ref, routes_ref, gates_ref, packed_ref):
    rows, width = tok_ref.shape
    experts = 32
    values = tok_ref[...].astype(jnp.float32)
    scaled = lax.rsqrt(jnp.mean(values * values, axis=-1, keepdims=True) + 1e-06)
    packed_ref[:, :width] = (values * scaled * gain_ref[...].astype(jnp.float32)[None, :]).astype(
        jnp.bfloat16
    )
    numbers = lax.broadcasted_iota(jnp.int32, (experts, rows), 0)
    chosen = jnp.zeros((experts, rows), jnp.float32)
    weight = jnp.zeros((experts, rows), jnp.float32)
    for k in range(routes_ref.shape[0]):
        hit = routes_ref[k : k + 1, :] == numbers
        chosen = jnp.where(hit, 1.0, chosen)
        weight = jnp.where(hit, gates_ref[k : k + 1, :].astype(jnp.float32), weight)
    row = lax.broadcasted_iota(jnp.int32, (rows, rows), 0)
    column = lax.broadcasted_iota(jnp.int32, (rows, rows), 1)
    upto = jnp.where(row <= column, 1.0, 0.0).astype(jnp.bfloat16)
    count = jnp.dot(chosen.astype(jnp.bfloat16), upto, preferred_element_type=jnp.float32)
    place = jnp.where(chosen > 0.5, count - 1.0, -1.0)
    packed_ref[:experts, width:] = place.astype(jnp.bfloat16)
    packed_ref[experts : 2 * experts, width:] = weight.astype(jnp.bfloat16)
    packed_ref[2 * experts :, width:] = jnp.zeros((rows - 2 * experts, rows), jnp.bfloat16)


def prepare(tokens, norm_gain, routes, route_gates):
    rows, width = tokens.shape
    return pl.pallas_call(
        prep_kernel,
        out_shape=jax.ShapeDtypeStruct((rows, width + rows), jnp.bfloat16),
        name="prepare",
    )(tokens, norm_gain, routes.T, route_gates.T)


def experts_kernel(
    ahead,
    first_ref,
    packed_hbm,
    gate_hbm,
    up_hbm,
    down_hbm,
    out_hbm,
    packed,
    gates,
    ups,
    downs,
    held,
    mix,
    incoming,
    outs,
    result,
    packed_sem,
    gate_sem,
    up_sem,
    down_sem,
    out_sem,
):
    experts, width, hidden = gate_hbm.shape
    sources = packed.shape[0]
    rows = packed.shape[1]
    numbered = held.shape[0]

    def load(hbm, buffer, sem, e):
        return pltpu.make_async_copy(hbm.at[e], buffer.at[e % 2], sem.at[e % 2])

    packed_in = [
        pltpu.make_async_copy(packed_hbm.at[pl.ds(s * rows, rows)], packed.at[s], packed_sem.at[s])
        for s in range(sources)
    ]
    for copy in packed_in:
        copy.start()
    gate_in = [load(gate_hbm, gates, gate_sem, e) for e in range(experts)]
    up_in = [load(up_hbm, ups, up_sem, e) for e in range(experts)]
    down_in = [load(down_hbm, downs, down_sem, e) for e in range(experts)]
    order = [copy for e in range(experts) for copy in (gate_in[e], up_in[e], down_in[e])]
    for copy in order[:ahead]:
        copy.start()

    def arrived(i):
        order[i].wait()
        if i + ahead < len(order):
            order[i + ahead].start()

    slots = lax.broadcasted_iota(jnp.int32, (CAP, rows), 0).astype(jnp.float32)
    for s in range(sources):
        packed_in[s].wait()
        held[...] = packed[s, :numbered, width:].astype(jnp.float32)
        picks = []
        for e in range(experts):
            place = held[pl.ds(first_ref[0] + e, 1), :]
            weight = held[pl.ds(first_ref[0] + numbered // 2 + e, 1), :]
            hit = place == slots
            picks.append(jnp.where(hit, 1.0, 0.0))
            mix[s, e * CAP : (e + 1) * CAP, :] = jnp.where(hit, weight, 0.0).astype(jnp.bfloat16)
        pick = jnp.concatenate(picks, axis=0).astype(jnp.bfloat16)
        chosen = jnp.dot(pick, packed[s, :, :width], preferred_element_type=jnp.float32)
        chosen = chosen.astype(jnp.bfloat16)
        for e in range(experts):
            incoming[e, s * CAP : (s + 1) * CAP, :] = chosen[e * CAP : (e + 1) * CAP]
    for e in range(experts):
        inputs = incoming[e]
        arrived(3 * e)
        gate = jnp.dot(inputs, gates[e % 2], preferred_element_type=jnp.float32)
        arrived(3 * e + 1)
        up = jnp.dot(inputs, ups[e % 2], preferred_element_type=jnp.float32)
        mid = (gate / (1.0 + jnp.exp(-gate)) * up).astype(jnp.bfloat16)
        arrived(3 * e + 2)
        out = jnp.dot(mid, downs[e % 2], preferred_element_type=jnp.float32).astype(jnp.bfloat16)
        for s in range(sources):
            outs[s, e * CAP : (e + 1) * CAP, :] = out[s * CAP : (s + 1) * CAP]
    sent = []
    for s in range(sources):
        result[s] = lax.dot_general(
            mix[s], outs[s], (((0,), (0,)), ((), ())), preferred_element_type=jnp.float32
        ).astype(jnp.bfloat16)
        copy = pltpu.make_async_copy(
            result.at[s], out_hbm.at[pl.ds(s * rows, rows)], out_sem.at[s]
        )
        copy.start()
        sent.append(copy)
    for copy in sent:
        copy.wait()


def run_experts(first, packed, gate, up, down, rows):
    experts, width, hidden = gate.shape
    sources = packed.shape[0] // rows
    anywhere = pl.BlockSpec(memory_space=pl.ANY)
    slots = sources * CAP
    return pl.pallas_call(
        functools.partial(experts_kernel, AHEAD),
        in_specs=[pl.BlockSpec(memory_space=pltpu.SMEM)] + [anywhere] * 4,
        out_specs=anywhere,
        out_shape=jax.ShapeDtypeStruct((sources * rows, width), jnp.bfloat16),
        scratch_shapes=[
            pltpu.VMEM((sources, rows, packed.shape[1]), jnp.bfloat16),
            pltpu.VMEM((2, width, hidden), jnp.bfloat16),
            pltpu.VMEM((2, width, hidden), jnp.bfloat16),
            pltpu.VMEM((2, hidden, width), jnp.bfloat16),
            pltpu.VMEM((64, rows), jnp.float32),
            pltpu.VMEM((sources, experts * CAP, rows), jnp.bfloat16),
            pltpu.VMEM((experts, slots, width), jnp.bfloat16),
            pltpu.VMEM((sources, experts * CAP, width), jnp.bfloat16),
            pltpu.VMEM((sources, rows, width), jnp.bfloat16),
            pltpu.SemaphoreType.DMA((sources,)),
            pltpu.SemaphoreType.DMA((2,)),
            pltpu.SemaphoreType.DMA((2,)),
            pltpu.SemaphoreType.DMA((2,)),
            pltpu.SemaphoreType.DMA((sources,)),
        ],
        compiler_params=pltpu.CompilerParams(vmem_limit_bytes=58 << 20),
        cost_estimate=pl.CostEstimate(
            flops=6 * experts * slots * width * hidden,
            bytes_accessed=6 * experts * width * hidden,
            transcendentals=experts * slots * hidden,
        ),
        name="run_experts",
    )(first, packed, gate, up, down)


def across(value, combine, axis, size):
    step = 1
    while step < size:
        pairs = [(i, i ^ step) for i in range(lax.axis_size(axis))]
        value = combine(value, lax.ppermute(value, axis, pairs))
        step *= 2
    return value


def total(value, axis, steps, size):
    sent = value.astype(jnp.bfloat16)
    got = [lax.ppermute(sent, axis, [(i, i ^ step) for i in range(size)]) for step in steps]
    for part in got:
        value = value + part.astype(jnp.float32)
    return value


def from_peer(value, step, size):
    return lax.ppermute(value, "dp", [(i, i ^ step) for i in range(size)])


def local_line(
    tokens,
    norm_gain,
    routes,
    route_gates,
    lengths,
    request_adapter,
    adapter_slot,
    expert_gate,
    expert_up,
    expert_down,
    shared_gate,
    shared_up_weight,
    shared_down,
    adapter_down,
    adapter_up,
    head_weight,
):
    tok_rows, width = tokens.shape
    tensor_size = lax.axis_size("tensor")
    data_size = lax.axis_size("dp")
    tensor_pos = lax.axis_index("tensor")
    data_pos = lax.axis_index("dp")
    experts = expert_gate.shape[0]
    packed = prepare(tokens, norm_gain, routes, route_gates)
    pooled = lax.all_gather(packed, "tensor", axis=0, tiled=True)
    normed = packed[:, :width]
    peers = [normed] + [from_peer(normed, d, data_size) for d in range(1, data_size)]
    peer_rows = jnp.concatenate(peers)
    block_rows = jnp.arange(tok_rows, dtype=jnp.int32)
    peer_dp = jnp.arange(data_size, dtype=jnp.int32) ^ data_pos
    bases = (peer_dp * tensor_size + tensor_pos) * tok_rows
    peer_positions = (bases[:, None] + block_rows[None, :]).reshape(-1)
    peer_slots = token_slots(peer_positions, lengths, request_adapter, adapter_slot)
    held_slots = peer_slots - data_pos * adapter_down.shape[0]
    peer_part = feed_forward(peer_rows, shared_gate, shared_up_weight, shared_down)
    peer_part = peer_part + adapter_delta(peer_rows, held_slots, adapter_down, adapter_up)
    peer_part = peer_part.astype(jnp.bfloat16)
    parts = peer_part.reshape(data_size, tok_rows, width)
    came = [from_peer(parts[d], d, data_size) for d in range(1, data_size)]
    first = (tensor_pos * experts).astype(jnp.int32).reshape(1)
    first, peer_part = lax.optimization_barrier((first, peer_part))
    partial = run_experts(first, pooled, expert_gate, expert_up, expert_down, tok_rows)
    partial, *came = lax.optimization_barrier((partial, *came))
    routed = lax.psum_scatter(partial, "tensor", scatter_dimension=0, tiled=True)
    ends = jnp.cumsum(lengths) - 1
    owner, row = ends // tok_rows, ends % tok_rows
    owner_dp, owner_tensor = owner // tensor_size, owner % tensor_size
    line_row = jnp.where(owner_dp == data_pos, owner_tensor * tok_rows + row, -1)
    peer_row = jnp.where(owner_tensor == tensor_pos, (owner_dp ^ data_pos) * tok_rows + row, -1)

    def pick(at, count):
        return jnp.where(
            at[:, None] == jnp.arange(count, dtype=jnp.int32)[None, :], 1.0, 0.0
        ).astype(jnp.bfloat16)

    last_part = jnp.dot(
        pick(line_row, tensor_size * tok_rows), partial, preferred_element_type=jnp.float32
    )
    last_part = last_part + jnp.dot(
        pick(peer_row, data_size * tok_rows), peer_part, preferred_element_type=jnp.float32
    )
    last = across(last_part, jnp.add, "tensor", 2)
    last = across(last, jnp.add, "dp", data_size)
    last = total(last, "tensor", range(2, tensor_size, 2), tensor_size).astype(jnp.bfloat16)
    last_values = last.astype(jnp.float32)
    last_norm = jnp.sqrt(jnp.sum(last_values * last_values, axis=1))
    logits = jnp.dot(last, head_weight, preferred_element_type=jnp.float32)
    block_logit = across(jnp.max(logits, axis=1, keepdims=True), jnp.maximum, "dp", data_size)
    out = routed.astype(jnp.float32) + parts[0].astype(jnp.float32)
    for part in came:
        out = out + part.astype(jnp.float32)
    return (out.astype(jnp.bfloat16), last_norm, block_logit)


def solution(mesh):
    placed = (
        P(("dp", "tensor"), None),
        P(),
        P(("dp", "tensor"), None),
        P(("dp", "tensor"), None),
        P(),
        P(),
        P(),
        P("tensor", None, None),
        P("tensor", None, None),
        P("tensor", None, None),
        P(None, "dp"),
        P(None, "dp"),
        P("dp", None),
        P("dp", None, None),
        P("dp", None, None),
        P(None, ("dp", "tensor")),
    )
    short = mesh.shape["tensor"] == 8 and mesh.shape["dp"] == 4
    return jax.shard_map(
        local_line if short else local,
        mesh=mesh,
        in_specs=placed,
        out_specs=(P(("dp", "tensor"), None), P(), P(None, "tensor")),
        check_vma=False,
    )
```

```python
import functools

import jax
import jax.numpy as jnp
from jax import lax
from jax.experimental import pallas as pl
from jax.experimental.pallas import tpu as pltpu
from jax.sharding import PartitionSpec as P

CAP = 32


def apply_norm(tokens, norm_gain):
    values = tokens.astype(jnp.float32)
    scaled = lax.rsqrt(jnp.mean(values * values, axis=-1, keepdims=True) + 1e-06)
    return (values * scaled * norm_gain.astype(jnp.float32)).astype(jnp.bfloat16)


def feed_forward(inputs, gate_mat, up_mat, down_mat):
    gate_portion = jnp.dot(inputs, gate_mat, preferred_element_type=jnp.float32)
    up_part = jnp.dot(inputs, up_mat, preferred_element_type=jnp.float32)
    hidden = (jax.nn.silu(gate_portion) * up_part).astype(jnp.bfloat16)
    return jnp.dot(hidden, down_mat, preferred_element_type=jnp.float32)


def token_slots(positions, lengths, request_adapter, adapter_slot):
    request_ends = jnp.cumsum(lengths)
    request = jnp.sum((request_ends[None, :] <= positions[:, None]).astype(jnp.int32), axis=1)
    request_pick = (
        request[:, None] == jnp.arange(request_adapter.shape[0], dtype=jnp.int32)[None, :]
    )
    adapter = jnp.sum(jnp.where(request_pick, request_adapter[None, :], 0), axis=1)
    adapter_pick = adapter[:, None] == jnp.arange(adapter_slot.shape[0], dtype=jnp.int32)[None, :]
    return jnp.sum(jnp.where(adapter_pick, adapter_slot[None, :], 0), axis=1)


def adapter_delta(inputs, slot_ids, down_store, up_store):
    held_count = down_store.shape[0]
    model_width = down_store.shape[1]
    rank_size = down_store.shape[2]
    flat_down = jnp.transpose(down_store, (1, 0, 2)).reshape(model_width, held_count * rank_size)
    low_rank = jnp.dot(inputs, flat_down, preferred_element_type=jnp.float32)
    low_rank = low_rank.reshape(inputs.shape[0], held_count, rank_size)
    keep_mask = slot_ids[:, None] == jnp.arange(held_count, dtype=jnp.int32)[None, :]
    low_rank = jnp.where(keep_mask[:, :, None], low_rank, 0.0).astype(jnp.bfloat16)
    low_rank = low_rank.reshape(inputs.shape[0], held_count * rank_size)
    flat_up = up_store.reshape(held_count * rank_size, up_store.shape[2])
    return jnp.dot(low_rank, flat_up, preferred_element_type=jnp.float32)


def local(
    tokens,
    norm_gain,
    routes,
    route_gates,
    lengths,
    request_adapter,
    adapter_slot,
    expert_gate,
    expert_up,
    expert_down,
    shared_gate,
    shared_up_weight,
    shared_down,
    adapter_down,
    adapter_up,
    head_weight,
):
    tok_rows = tokens.shape[0]
    model_width = tokens.shape[1]
    route_count = routes.shape[1]
    tensor_size = lax.axis_size("tensor")
    tensor_pos = lax.axis_index("tensor")
    data_pos = lax.axis_index("dp")
    local_experts = expert_gate.shape[0]
    all_experts = local_experts * tensor_size
    slot_range = jnp.arange(CAP, dtype=jnp.int32)
    normed = apply_norm(tokens, norm_gain)
    numbers = jnp.arange(all_experts, dtype=jnp.int32)
    route_hits = routes[:, :, None] == numbers[None, None, :]
    chosen = jnp.any(route_hits, axis=1)
    weight = jnp.sum(
        jnp.where(route_hits, route_gates[:, :, None], jnp.zeros((), jnp.bfloat16)), axis=1
    )
    slot_place = jnp.cumsum(chosen.astype(jnp.int32), axis=0) - 1
    pooled, pooled_routes = (
        lax.all_gather(normed, "tensor", axis=0, tiled=True),
        lax.all_gather(routes.astype(jnp.bfloat16), "tensor", axis=0, tiled=True),
    )
    pooled = pooled.reshape(tensor_size, tok_rows, model_width)
    source_routes = pooled_routes.astype(jnp.int32).reshape(tensor_size, tok_rows, route_count)
    own_numbers = tensor_pos * local_experts + jnp.arange(local_experts, dtype=jnp.int32)
    source_hits = source_routes[:, :, :, None] == own_numbers[None, None, None, :]
    source_chosen = jnp.any(source_hits, axis=2)
    source_place = jnp.cumsum(source_chosen.astype(jnp.int32), axis=1) - 1
    source_pick = source_chosen[:, :, :, None] & (
        source_place[:, :, :, None] == slot_range[None, None, None, :]
    )
    source_pick = jnp.where(source_pick, 1.0, 0.0).astype(jnp.bfloat16)
    incoming = jnp.einsum(
        "sijc,sid->sjcd", source_pick, pooled, preferred_element_type=jnp.float32
    ).astype(jnp.bfloat16)
    gate_portion = jnp.einsum(
        "secd,edf->secf", incoming, expert_gate, preferred_element_type=jnp.float32
    )
    up_part = jnp.einsum("secd,edf->secf", incoming, expert_up, preferred_element_type=jnp.float32)
    hidden = (jax.nn.silu(gate_portion) * up_part).astype(jnp.bfloat16)
    expert_out = jnp.einsum(
        "secf,efd->secd", hidden, expert_down, preferred_element_type=jnp.float32
    ).astype(jnp.bfloat16)
    returned_rows = lax.all_to_all(expert_out, "tensor", split_axis=0, concat_axis=0, tiled=True)
    returned_rows = returned_rows.reshape(all_experts, CAP, model_width)
    mixing_result = jnp.where(
        slot_place[:, :, None] == slot_range[None, None, :],
        weight[:, :, None],
        jnp.zeros((), jnp.bfloat16),
    )
    routed_output = jnp.einsum(
        "kbt,btw->kw", mixing_result, returned_rows, preferred_element_type=jnp.float32
    )
    own_base = (data_pos * tensor_size + tensor_pos) * tok_rows
    own_positions = own_base + jnp.arange(tok_rows, dtype=jnp.int32)
    peer_rows = lax.all_gather(normed, "dp", axis=0, tiled=True)
    shared_sum = lax.psum_scatter(
        feed_forward(peer_rows, shared_gate, shared_up_weight, shared_down),
        "dp",
        scatter_dimension=0,
        tiled=True,
    )
    own_slots = token_slots(own_positions, lengths, request_adapter, adapter_slot)
    store_down, store_up = (
        lax.all_gather(adapter_down, "dp", axis=0, tiled=True),
        lax.all_gather(adapter_up, "dp", axis=0, tiled=True),
    )
    summed = routed_output + shared_sum + adapter_delta(normed, own_slots, store_down, store_up)
    sublayer_out = summed.astype(jnp.bfloat16)
    request_ends = jnp.cumsum(lengths)
    last_pick = jnp.where(request_ends[:, None] - 1 == own_positions[None, :], 1.0, 0.0).astype(
        jnp.bfloat16
    )
    last_part = jnp.dot(last_pick, sublayer_out, preferred_element_type=jnp.float32)
    last_states = lax.psum(last_part, ("dp", "tensor"))
    last_norm = jnp.sqrt(jnp.sum(last_states * last_states, axis=1))
    logits = jnp.dot(
        last_states.astype(jnp.bfloat16), head_weight, preferred_element_type=jnp.float32
    )
    block_logit = lax.pmax(jnp.max(logits, axis=1), "dp")
    return (sublayer_out, last_norm, block_logit[:, None])


AHEAD = 3
RANK = 16


def scaled_rows(tokens, gain):
    values = tokens.astype(jnp.float32)
    scaled = lax.rsqrt(jnp.mean(values * values, axis=-1, keepdims=True) + 1e-06)
    return (values * scaled * gain).astype(jnp.bfloat16)


def prep_kernel(
    tok_ref, twin_ref, gain_ref, routes_ref, twin_routes_ref, gates_ref, twin_gates_ref, *outs
):
    first_ref, second_ref, whole_ref = outs
    rows, width = tok_ref.shape
    half = width // 2
    experts = 32
    row = lax.broadcasted_iota(jnp.int32, (rows, rows), 0)
    column = lax.broadcasted_iota(jnp.int32, (rows, rows), 1)
    upto = jnp.where(row <= column, 1.0, 0.0).astype(jnp.bfloat16)
    numbers = lax.broadcasted_iota(jnp.int32, (experts, rows), 0)
    gain = gain_ref[...].astype(jnp.float32)[None, :]
    own = (tok_ref, routes_ref, gates_ref)
    twin = (twin_ref, twin_routes_ref, twin_gates_ref)
    for c, (tokens, routes, gates) in enumerate((own, twin)):
        at = c * rows
        normed = scaled_rows(tokens[...], gain)
        if c == 0:
            whole_ref[...] = normed
        first_ref[at : at + rows, :half] = normed[:, :half]
        second_ref[at : at + rows, :] = normed[:, half:]
        chosen = jnp.zeros((experts, rows), jnp.float32)
        weight = jnp.zeros((experts, rows), jnp.float32)
        for k in range(routes.shape[0]):
            hit = routes[k : k + 1, :] == numbers
            chosen = jnp.where(hit, 1.0, chosen)
            weight = jnp.where(hit, gates[k : k + 1, :].astype(jnp.float32), weight)
        count = jnp.dot(chosen.astype(jnp.bfloat16), upto, preferred_element_type=jnp.float32)
        place = jnp.where(chosen > 0.5, count - 1.0, -1.0)
        first_ref[at : at + experts, half:] = place.astype(jnp.bfloat16)
        first_ref[at + experts : at + 2 * experts, half:] = weight.astype(jnp.bfloat16)
        first_ref[at + 2 * experts : at + rows, half:] = jnp.zeros(
            (rows - 2 * experts, rows), jnp.bfloat16
        )


def prepare(tokens, twin, norm_gain, routes, twin_routes, gates, twin_gates):
    rows, width = tokens.shape
    half = width // 2
    return pl.pallas_call(
        prep_kernel,
        out_shape=(
            jax.ShapeDtypeStruct((2 * rows, half + rows), jnp.bfloat16),
            jax.ShapeDtypeStruct((2 * rows, half), jnp.bfloat16),
            jax.ShapeDtypeStruct((rows, width), jnp.bfloat16),
        ),
        name="prepare",
    )(tokens, twin, norm_gain, routes, twin_routes, gates, twin_gates)


def across_columns(left, right):
    return lax.dot_general(left, right, (((1,), (1,)), ((), ())), preferred_element_type=jnp.float32)


def experts_kernel(ahead, chips, count, position_ref, last_ref, slots_ref, peer_last_ref, *refs):
    arrivals = 2 * chips - 1
    shared_hbm, peers_hbm, refs = refs[:5], refs[5 : 6 + count], refs[6 + count :]
    left_hbm, right_hbm, refs = refs[:arrivals], refs[arrivals : 2 * arrivals], refs[2 * arrivals :]
    gate_hbm, up_hbm, down_hbm, refs = *refs[:3], refs[3:]
    left_out, right_out, last_out = refs[:chips], refs[chips : 2 * chips], refs[2 * chips]
    parts_hbm, refs = refs[2 * chips + 1 : 2 * chips + 2 + count], refs[2 * chips + 2 + count :]
    left, right, gates, ups, downs, held, mix, incoming, outs, result = refs[:10]
    left_sem, right_sem, gate_sem, up_sem, down_sem, left_out_sem, right_out_sem = refs[10:17]
    shared_sem, peer_sem, part_sem = refs[17:]
    experts, width, hidden = gate_hbm.shape
    rows = left.shape[1] // 2
    half = width // 2
    numbered = held.shape[0]
    first = position_ref[0] * experts

    def load(hbm, buffer, sem, e):
        return pltpu.make_async_copy(hbm.at[e], buffer.at[e % 2], sem.at[e % 2])

    sides = ((left_hbm, left, left_sem), (right_hbm, right, right_sem))

    def fetch(side, d):
        hbm, buffer, sem = side
        return pltpu.make_async_copy(hbm[d], buffer.at[d], sem.at[d])

    def fetch_swapped(side, d):
        hbm, buffer, sem = side
        for c in range(2):
            pltpu.make_async_copy(
                hbm[arrivals - d].at[pl.ds((1 - c) * rows, rows)],
                buffer.at[d, pl.ds(c * rows, rows)],
                sem.at[d],
            ).start()

    chip, core = lax.div(position_ref[0], 2), lax.rem(position_ref[0], 2)
    for d in range(chips):
        near = (core == 0) & (chip >= d) | (core == 1) & (chip + d < chips)
        for side in sides:
            if d == 0:
                fetch(side, d).start()
            else:
                pl.when(near)(lambda: fetch(side, d).start())
                pl.when(jnp.logical_not(near))(lambda: fetch_swapped(side, d))
    gate_in = [load(gate_hbm, gates, gate_sem, e) for e in range(experts)]
    up_in = [load(up_hbm, ups, up_sem, e) for e in range(experts)]
    down_in = [load(down_hbm, downs, down_sem, e) for e in range(experts)]
    order = [copy for e in range(experts) for copy in (gate_in[e], up_in[e], down_in[e])]
    for copy in order[:ahead]:
        copy.start()

    def arrived(i):
        order[i].wait()
        if i + ahead < len(order):
            order[i + ahead].start()

    per = incoming.shape[1] // rows
    peer_in = []
    for p in range(count + 1):
        q = min(p, count - 1)
        to = incoming.at[q // per, pl.ds(q % per * rows, rows)]
        if p >= count - 1:
            to = to.at[:, pl.ds((p - count + 1) * half, half)]
        peer_in.append(pltpu.make_async_copy(peers_hbm[p], to, peer_sem.at[p]))
    begins = [0]
    for hbm in shared_hbm:
        begins.append(begins[-1] + hbm.shape[0])
    shared_in = [
        pltpu.make_async_copy(
            hbm, downs.at[0, pl.ds(begin, hbm.shape[0])], shared_sem.at[i]
        )
        for i, (hbm, begin) in enumerate(zip(shared_hbm, begins))
    ]
    slots = lax.broadcasted_iota(jnp.int32, (CAP, rows), 0).astype(jnp.float32)
    for d in range(chips):
        for side in sides:
            fetch(side, d).wait()
        for c in range(2):
            s = 2 * d + c
            own = pl.ds(c * rows, rows)
            held[...] = left[d, pl.ds(c * rows, numbered), half:].astype(jnp.float32)
            picks = []
            for e in range(experts):
                place = held[pl.ds(first + e, 1), :]
                weight = held[pl.ds(first + numbered // 2 + e, 1), :]
                hit = place == slots
                picks.append(jnp.where(hit, 1.0, 0.0))
                mix[s, e * CAP : (e + 1) * CAP, :] = jnp.where(hit, weight, 0.0).astype(
                    jnp.bfloat16
                )
            pick = jnp.concatenate(picks, axis=0).astype(jnp.bfloat16)
            for ref, to in ((left, 0), (right, half)):
                chosen = jnp.dot(pick, ref[d, own, :half], preferred_element_type=jnp.float32)
                chosen = chosen.astype(jnp.bfloat16)
                for e in range(experts):
                    incoming[e, s * CAP : (s + 1) * CAP, to : to + half] = chosen[
                        e * CAP : (e + 1) * CAP
                    ]
    for e in range(experts):
        inputs = incoming[e]
        arrived(3 * e)
        gate = jnp.dot(inputs, gates[e % 2], preferred_element_type=jnp.float32)
        arrived(3 * e + 1)
        up = jnp.dot(inputs, ups[e % 2], preferred_element_type=jnp.float32)
        mid = (gate / (1.0 + jnp.exp(-gate)) * up).astype(jnp.bfloat16)
        arrived(3 * e + 2)
        out = jnp.dot(mid, downs[e % 2], preferred_element_type=jnp.float32).astype(jnp.bfloat16)
        for s in range(2 * chips):
            outs[s, e * CAP : (e + 1) * CAP, :] = out[s * CAP : (s + 1) * CAP]
        if e == experts - 2:
            for copy in peer_in + shared_in:
                copy.start()
    sent = []
    for d in range(chips):
        for c in range(2):
            result[d, c * rows : (c + 1) * rows, :] = lax.dot_general(
                mix[2 * d + c],
                outs[2 * d + c],
                (((0,), (0,)), ((), ())),
                preferred_element_type=jnp.float32,
            ).astype(jnp.bfloat16)
        sent.append(
            pltpu.make_async_copy(result.at[d, :, :half], left_out[d], left_out_sem.at[d])
        )
        sent.append(
            pltpu.make_async_copy(result.at[d, :, half:], right_out[d], right_out_sem.at[d])
        )
        sent[-2].start()
        sent[-1].start()
    for copy in peer_in + shared_in:
        copy.wait()
    gate_ref, up_ref, down_ref, lower_ref, upper_ref = [
        downs.at[0, pl.ds(begin, hbm.shape[0])] for hbm, begin in zip(shared_hbm, begins)
    ]
    batch = incoming.shape[1]
    at = lax.broadcasted_iota(jnp.int32, (last_ref.shape[0], batch), 1)
    last = None
    for b in range(count // per):
        inputs = incoming[b]
        gate = across_columns(inputs, gate_ref[...])
        up = across_columns(inputs, up_ref[...])
        mid = (gate / (1.0 + jnp.exp(-gate)) * up).astype(jnp.bfloat16)
        low = across_columns(inputs, lower_ref[...])
        slot = slots_ref[b * batch : (b + 1) * batch, :]
        place = lax.broadcasted_iota(jnp.int32, low.shape, 1) - slot * RANK
        low = jnp.where((place >= 0) & (place < RANK), low, 0.0).astype(jnp.bfloat16)
        part = jnp.dot(mid, down_ref[...], preferred_element_type=jnp.float32)
        part = part + jnp.dot(low, upper_ref[...], preferred_element_type=jnp.float32)
        part = part.astype(jnp.bfloat16)
        store = experts - count // per + b
        incoming[store] = part
        for c in range(per):
            p = per * b + c
            value = incoming.at[store, pl.ds(c * rows, rows)]
            values = [value]
            if p == count - 1:
                values = [value.at[:, pl.ds(0, half)], value.at[:, pl.ds(half, half)]]
            for i, value in enumerate(values):
                sent.append(pltpu.make_async_copy(value, parts_hbm[p + i], part_sem.at[p + i]))
                sent[-1].start()
        pick = jnp.where(peer_last_ref[...] - b * batch == at, 1.0, 0.0).astype(jnp.bfloat16)
        term = jnp.dot(pick, part, preferred_element_type=jnp.float32)
        last = term if last is None else last + term
    at = lax.broadcasted_iota(jnp.int32, (last_ref.shape[0], 2 * rows), 1)
    for d in range(chips):
        pick = jnp.where(last_ref[...] - d * 2 * rows == at, 1.0, 0.0).astype(jnp.bfloat16)
        last = last + jnp.dot(pick, result[d], preferred_element_type=jnp.float32)
    last_out[...] = last[: last_out.shape[0]]
    for copy in sent:
        copy.wait()


def run_experts(
    position, last_at, slots_at, peer_last, shared, peers, left, right, gate, up, down, requests
):
    experts, width, hidden = gate.shape
    arrivals = len(left)
    count = len(peers) - 1
    chips = (arrivals + 1) // 2
    both = left[0].shape[0]
    rows = both // 2
    half = width // 2
    slots = 2 * chips * CAP
    anywhere = pl.BlockSpec(memory_space=pltpu.MemorySpace.HBM)
    inside = pl.BlockSpec(memory_space=pltpu.VMEM)
    passed = jax.ShapeDtypeStruct((both, half), jnp.bfloat16)
    return pl.pallas_call(
        functools.partial(experts_kernel, AHEAD, chips, count),
        in_specs=[pl.BlockSpec(memory_space=pltpu.SMEM)]
        + [inside] * 3
        + [anywhere] * (6 + count + 2 * arrivals + 3),
        out_specs=[anywhere] * (2 * chips) + [inside] + [anywhere] * (count + 1),
        out_shape=[passed] * (2 * chips)
        + [jax.ShapeDtypeStruct((requests, width), jnp.float32)]
        + [jax.ShapeDtypeStruct((rows, width), jnp.bfloat16)] * (count - 1)
        + [jax.ShapeDtypeStruct((rows, half), jnp.bfloat16)] * 2,
        scratch_shapes=[
            pltpu.VMEM((chips, both, half + rows), jnp.bfloat16),
            pltpu.VMEM((chips, both, half), jnp.bfloat16),
            pltpu.VMEM((2, width, hidden), jnp.bfloat16),
            pltpu.VMEM((2, width, hidden), jnp.bfloat16),
            pltpu.VMEM((2, hidden, width), jnp.bfloat16),
            pltpu.VMEM((64, rows), jnp.float32),
            pltpu.VMEM((2 * chips, experts * CAP, rows), jnp.bfloat16),
            pltpu.VMEM((experts, slots, width), jnp.bfloat16),
            pltpu.VMEM((2 * chips, experts * CAP, width), jnp.bfloat16),
            pltpu.VMEM((chips, both, width), jnp.bfloat16),
            pltpu.SemaphoreType.DMA((chips,)),
            pltpu.SemaphoreType.DMA((chips,)),
            pltpu.SemaphoreType.DMA((2,)),
            pltpu.SemaphoreType.DMA((2,)),
            pltpu.SemaphoreType.DMA((2,)),
            pltpu.SemaphoreType.DMA((chips,)),
            pltpu.SemaphoreType.DMA((chips,)),
            pltpu.SemaphoreType.DMA((5,)),
            pltpu.SemaphoreType.DMA((count + 1,)),
            pltpu.SemaphoreType.DMA((count + 1,)),
        ],
        compiler_params=pltpu.CompilerParams(vmem_limit_bytes=60 << 20),
        cost_estimate=pl.CostEstimate(
            flops=6 * experts * slots * width * hidden,
            bytes_accessed=6 * experts * width * hidden,
            transcendentals=experts * slots * hidden,
        ),
        name="run_experts",
    )(position, last_at, slots_at, peer_last, *shared, *peers, *left, *right, gate, up, down)


def add(*terms):
    total = terms[0].astype(jnp.float32)
    for term in terms[1:]:
        total = total + term.astype(jnp.float32)
    return total.astype(jnp.bfloat16)


def swapped(value):
    rows = value.shape[0] // 2
    return jnp.concatenate([value[rows:], value[:rows]])


def twin_of(value, tensor_size):
    return lax.ppermute(value, "tensor", [(i, i ^ 1) for i in range(tensor_size)])


def along(value, chips, distance, begin=0, end=None):
    end = chips - distance if end is None else end
    upward = [(2 * z, 2 * (z + distance)) for z in range(begin, end)]
    downward = [
        (2 * (chips - 1 - z) + 1, 2 * (chips - 1 - z - distance) + 1) for z in range(begin, end)
    ]
    return lax.ppermute(value, "tensor", upward + downward)


def spread(chunks, chips):
    groups = [[chunk] for chunk in chunks]
    for k in range(1, chips):
        for group in groups:
            group.append(along(group[-1], chips, 1, k - 1))
    return groups


def collect(parts, chips, begin):
    run = [None] * len(parts)
    rows = parts[0][0].shape[0]
    for k in range(1, chips):
        for j, part in enumerate(parts):
            got = swapped(twin_of(part[chips - k], 2 * chips))
            terms = (part[k], got) if run[j] is None else (part[k], got, run[j][:rows])
            sent = add(*terms)
            if k == 1 and j == 0:
                carried, came = begin(sent)
                carry = carried
            if k == chips - 1 and j == len(parts) - 1:
                sent, *came = lax.optimization_barrier((sent, *came))
            if j == len(parts) - 1:
                if k > 1:
                    carry = add(carried, run[j][rows:])
                sent = jnp.concatenate([sent, carry])
            run[j] = along(sent, chips, 1, 0, k)
    done = []
    for j, part in enumerate(parts):
        total = add(part[0], run[j][:rows])
        own, other = total[: rows // 2], total[rows // 2 :]
        if j == len(parts) - 1:
            other = jnp.concatenate([other, run[j][rows:]])
        got = twin_of(other, 2 * chips)
        done.append((own, got[: rows // 2]))
    return done, came, [carried, run[-1][rows:], got[rows // 2 :]]


def across(value, combine, axis, size):
    step = 1
    while step < size:
        pairs = [(i, i ^ step) for i in range(lax.axis_size(axis))]
        value = combine(value, lax.ppermute(value, axis, pairs))
        step *= 2
    return value


def sent_along(value, axis, steps, size):
    return [lax.ppermute(value, axis, [(i, i ^ step) for i in range(size)]) for step in steps]


def after(values, other):
    *values, _ = lax.optimization_barrier((*values, other))
    return values


def summed(values):
    result = values[0].astype(jnp.float32)
    for value in values[1:]:
        result = result + value.astype(jnp.float32)
    return result


def from_peer(value, step, size):
    return lax.ppermute(value, "dp", [(i, i ^ step) for i in range(size)])


def local_line(
    tokens,
    norm_gain,
    routes,
    route_gates,
    lengths,
    request_adapter,
    adapter_slot,
    expert_gate,
    expert_up,
    expert_down,
    shared_gate,
    shared_up_weight,
    shared_down,
    adapter_down,
    adapter_up,
    head_weight,
):
    tok_rows, width = tokens.shape
    tensor_size = lax.axis_size("tensor")
    data_size = lax.axis_size("dp")
    tensor_pos = lax.axis_index("tensor")
    data_pos = lax.axis_index("dp")
    chips = tensor_size // 2
    small = (routes.T, route_gates.T)
    own = (tokens, *small)
    twin = [twin_of(value, tensor_size) for value in own]
    first, second, normed = prepare(
        tokens, twin[0], norm_gain, small[0], twin[1], small[1], twin[2]
    )
    left, right = spread([first, second], chips)
    near = [from_peer(normed, d, data_size) for d in (1, 2)]
    peers = [
        normed,
        *near,
        from_peer(near[1][:, : width // 2], 1, data_size),
        from_peer(near[0][:, width // 2 :], 2, data_size),
    ]
    block_rows = jnp.arange(tok_rows, dtype=jnp.int32)
    peer_dp = jnp.arange(data_size, dtype=jnp.int32) ^ data_pos
    bases = (peer_dp * tensor_size + tensor_pos) * tok_rows
    peer_positions = (bases[:, None] + block_rows[None, :]).reshape(-1)
    peer_slots = token_slots(peer_positions, lengths, request_adapter, adapter_slot)
    held_count, _, rank = adapter_down.shape
    held_slots = (peer_slots - data_pos * held_count)[:, None]
    lower = jnp.transpose(adapter_down, (0, 2, 1)).reshape(held_count * rank, width)
    upper = adapter_up.reshape(held_count * rank, width)
    ends = jnp.cumsum(lengths) - 1
    owner, row = ends // tok_rows, ends % tok_rows
    owner_dp, owner_tensor = owner // tensor_size, owner % tensor_size
    requests = ends.shape[0]
    chip, core = tensor_pos // 2, tensor_pos % 2
    steps = jnp.where(core == 0, chip - owner_tensor // 2, owner_tensor // 2 - chip) % chips
    away = (2 * steps + (owner_tensor % 2 != core)) * tok_rows + row
    line_at = jnp.where(owner_dp == data_pos, away, -1)
    across_at = (owner_dp ^ data_pos) * tok_rows + row
    peer_at = jnp.where(owner_tensor == tensor_pos, across_at, -1)
    padding = ((0, -requests % 16), (0, 0))
    line_at = jnp.pad(line_at[:, None], padding, constant_values=-1)
    peer_at = jnp.pad(peer_at[:, None], padding, constant_values=-1)
    early = after(left[1:-1] + right[1:-1], right[-2])
    early = [early[: chips - 2], early[chips - 2 :]]
    left = left + [twin_of(part, tensor_size) for part in early[0] + left[-1:]]
    right = right + [twin_of(part, tensor_size) for part in early[1] + right[-1:]]
    results = run_experts(
        tensor_pos.astype(jnp.int32).reshape(1),
        line_at,
        held_slots,
        peer_at,
        [shared_gate.T, shared_up_weight.T, shared_down, lower, upper],
        peers,
        left,
        right,
        expert_gate,
        expert_up,
        expert_down,
        requests,
    )
    passed, last, parts = results[: 2 * chips], results[2 * chips], results[2 * chips + 1 :]
    half = width // 2

    def begin(ready):
        value, *tied = after([last, *parts], ready)
        value = across(value, jnp.add, "tensor", 2)
        sent = value.astype(jnp.bfloat16)
        value = summed([value] + sent_along(sent, "dp", range(1, data_size), data_size))
        far = [from_peer(tied[3], 1, data_size), from_peer(tied[4], 2, data_size)]
        joined = [
            jnp.concatenate([tied[1][:, :half], add(tied[1][:, half:], far[1])], axis=1),
            jnp.concatenate([add(tied[2][:, :half], far[0]), tied[2][:, half:]], axis=1),
        ]
        came = [from_peer(joined[0], 1, data_size), from_peer(joined[1], 2, data_size)]
        value = value.astype(jnp.bfloat16)
        return jnp.concatenate([value[:, :half], value[:, half:]]), came

    routed, came, carried = collect([passed[:chips], passed[chips:]], chips, begin)
    last = summed(carried)
    last = jnp.concatenate([last[:requests], last[requests:]], axis=1).astype(jnp.bfloat16)
    last_values = last.astype(jnp.float32)
    last_norm = jnp.sqrt(jnp.sum(last_values * last_values, axis=1))
    logits = jnp.dot(last, head_weight, preferred_element_type=jnp.float32)
    top = jnp.max(logits, axis=1, keepdims=True)
    tops = [top] + sent_along(top, "dp", range(1, data_size), data_size)
    block_logit = functools.reduce(jnp.maximum, tops)
    out = jnp.concatenate([a.astype(jnp.float32) + b.astype(jnp.float32) for a, b in routed], axis=1)
    out = out + summed([parts[0], *came])
    return (out.astype(jnp.bfloat16), last_norm, block_logit)


def solution(mesh):
    placed = (
        P(("dp", "tensor"), None),
        P(),
        P(("dp", "tensor"), None),
        P(("dp", "tensor"), None),
        P(),
        P(),
        P(),
        P("tensor", None, None),
        P("tensor", None, None),
        P("tensor", None, None),
        P(None, "dp"),
        P(None, "dp"),
        P("dp", None),
        P("dp", None, None),
        P("dp", None, None),
        P(None, ("dp", "tensor")),
    )
    short = mesh.shape["tensor"] == 8 and mesh.shape["dp"] == 4
    return jax.shard_map(
        local_line if short else local,
        mesh=mesh,
        in_specs=placed,
        out_specs=(P(("dp", "tensor"), None), P(), P(None, "tensor")),
        check_vma=False,
    )
```

```python
import functools

import jax
import jax.numpy as jnp
from jax import lax
from jax.experimental import pallas as pl
from jax.experimental.pallas import tpu as pltpu
from jax.sharding import PartitionSpec as P

CAP = 32


def apply_norm(tokens, norm_gain):
    values = tokens.astype(jnp.float32)
    scaled = lax.rsqrt(jnp.mean(values * values, axis=-1, keepdims=True) + 1e-06)
    return (values * scaled * norm_gain.astype(jnp.float32)).astype(jnp.bfloat16)


def feed_forward(inputs, gate_mat, up_mat, down_mat):
    gate_portion = jnp.dot(inputs, gate_mat, preferred_element_type=jnp.float32)
    up_part = jnp.dot(inputs, up_mat, preferred_element_type=jnp.float32)
    hidden = (jax.nn.silu(gate_portion) * up_part).astype(jnp.bfloat16)
    return jnp.dot(hidden, down_mat, preferred_element_type=jnp.float32)


def token_slots(positions, lengths, request_adapter, adapter_slot):
    request_ends = jnp.cumsum(lengths)
    request = jnp.sum((request_ends[None, :] <= positions[:, None]).astype(jnp.int32), axis=1)
    request_pick = (
        request[:, None] == jnp.arange(request_adapter.shape[0], dtype=jnp.int32)[None, :]
    )
    adapter = jnp.sum(jnp.where(request_pick, request_adapter[None, :], 0), axis=1)
    adapter_pick = adapter[:, None] == jnp.arange(adapter_slot.shape[0], dtype=jnp.int32)[None, :]
    return jnp.sum(jnp.where(adapter_pick, adapter_slot[None, :], 0), axis=1)


def adapter_delta(inputs, slot_ids, down_store, up_store):
    held_count = down_store.shape[0]
    model_width = down_store.shape[1]
    rank_size = down_store.shape[2]
    flat_down = jnp.transpose(down_store, (1, 0, 2)).reshape(model_width, held_count * rank_size)
    low_rank = jnp.dot(inputs, flat_down, preferred_element_type=jnp.float32)
    low_rank = low_rank.reshape(inputs.shape[0], held_count, rank_size)
    keep_mask = slot_ids[:, None] == jnp.arange(held_count, dtype=jnp.int32)[None, :]
    low_rank = jnp.where(keep_mask[:, :, None], low_rank, 0.0).astype(jnp.bfloat16)
    low_rank = low_rank.reshape(inputs.shape[0], held_count * rank_size)
    flat_up = up_store.reshape(held_count * rank_size, up_store.shape[2])
    return jnp.dot(low_rank, flat_up, preferred_element_type=jnp.float32)


def local(
    tokens,
    norm_gain,
    routes,
    route_gates,
    lengths,
    request_adapter,
    adapter_slot,
    expert_gate,
    expert_up,
    expert_down,
    shared_gate,
    shared_up_weight,
    shared_down,
    adapter_down,
    adapter_up,
    head_weight,
):
    tok_rows = tokens.shape[0]
    model_width = tokens.shape[1]
    route_count = routes.shape[1]
    tensor_size = lax.axis_size("tensor")
    tensor_pos = lax.axis_index("tensor")
    data_pos = lax.axis_index("dp")
    local_experts = expert_gate.shape[0]
    all_experts = local_experts * tensor_size
    slot_range = jnp.arange(CAP, dtype=jnp.int32)
    normed = apply_norm(tokens, norm_gain)
    numbers = jnp.arange(all_experts, dtype=jnp.int32)
    route_hits = routes[:, :, None] == numbers[None, None, :]
    chosen = jnp.any(route_hits, axis=1)
    weight = jnp.sum(
        jnp.where(route_hits, route_gates[:, :, None], jnp.zeros((), jnp.bfloat16)), axis=1
    )
    slot_place = jnp.cumsum(chosen.astype(jnp.int32), axis=0) - 1
    pooled, pooled_routes = (
        lax.all_gather(normed, "tensor", axis=0, tiled=True),
        lax.all_gather(routes.astype(jnp.bfloat16), "tensor", axis=0, tiled=True),
    )
    pooled = pooled.reshape(tensor_size, tok_rows, model_width)
    source_routes = pooled_routes.astype(jnp.int32).reshape(tensor_size, tok_rows, route_count)
    own_numbers = tensor_pos * local_experts + jnp.arange(local_experts, dtype=jnp.int32)
    source_hits = source_routes[:, :, :, None] == own_numbers[None, None, None, :]
    source_chosen = jnp.any(source_hits, axis=2)
    source_place = jnp.cumsum(source_chosen.astype(jnp.int32), axis=1) - 1
    source_pick = source_chosen[:, :, :, None] & (
        source_place[:, :, :, None] == slot_range[None, None, None, :]
    )
    source_pick = jnp.where(source_pick, 1.0, 0.0).astype(jnp.bfloat16)
    incoming = jnp.einsum(
        "sijc,sid->sjcd", source_pick, pooled, preferred_element_type=jnp.float32
    ).astype(jnp.bfloat16)
    gate_portion = jnp.einsum(
        "secd,edf->secf", incoming, expert_gate, preferred_element_type=jnp.float32
    )
    up_part = jnp.einsum("secd,edf->secf", incoming, expert_up, preferred_element_type=jnp.float32)
    hidden = (jax.nn.silu(gate_portion) * up_part).astype(jnp.bfloat16)
    expert_out = jnp.einsum(
        "secf,efd->secd", hidden, expert_down, preferred_element_type=jnp.float32
    ).astype(jnp.bfloat16)
    returned_rows = lax.all_to_all(expert_out, "tensor", split_axis=0, concat_axis=0, tiled=True)
    returned_rows = returned_rows.reshape(all_experts, CAP, model_width)
    mixing_result = jnp.where(
        slot_place[:, :, None] == slot_range[None, None, :],
        weight[:, :, None],
        jnp.zeros((), jnp.bfloat16),
    )
    routed_output = jnp.einsum(
        "kbt,btw->kw", mixing_result, returned_rows, preferred_element_type=jnp.float32
    )
    own_base = (data_pos * tensor_size + tensor_pos) * tok_rows
    own_positions = own_base + jnp.arange(tok_rows, dtype=jnp.int32)
    peer_rows = lax.all_gather(normed, "dp", axis=0, tiled=True)
    shared_sum = lax.psum_scatter(
        feed_forward(peer_rows, shared_gate, shared_up_weight, shared_down),
        "dp",
        scatter_dimension=0,
        tiled=True,
    )
    own_slots = token_slots(own_positions, lengths, request_adapter, adapter_slot)
    store_down, store_up = (
        lax.all_gather(adapter_down, "dp", axis=0, tiled=True),
        lax.all_gather(adapter_up, "dp", axis=0, tiled=True),
    )
    summed = routed_output + shared_sum + adapter_delta(normed, own_slots, store_down, store_up)
    sublayer_out = summed.astype(jnp.bfloat16)
    request_ends = jnp.cumsum(lengths)
    last_pick = jnp.where(request_ends[:, None] - 1 == own_positions[None, :], 1.0, 0.0).astype(
        jnp.bfloat16
    )
    last_part = jnp.dot(last_pick, sublayer_out, preferred_element_type=jnp.float32)
    last_states = lax.psum(last_part, ("dp", "tensor"))
    last_norm = jnp.sqrt(jnp.sum(last_states * last_states, axis=1))
    logits = jnp.dot(
        last_states.astype(jnp.bfloat16), head_weight, preferred_element_type=jnp.float32
    )
    block_logit = lax.pmax(jnp.max(logits, axis=1), "dp")
    return (sublayer_out, last_norm, block_logit[:, None])


AHEAD = 3
RANK = 16


def scaled_rows(tokens, gain):
    values = tokens.astype(jnp.float32)
    scaled = lax.rsqrt(jnp.mean(values * values, axis=-1, keepdims=True) + 1e-06)
    return (values * scaled * gain).astype(jnp.bfloat16)


def prep_kernel(
    tok_ref, twin_ref, gain_ref, routes_ref, twin_routes_ref, gates_ref, twin_gates_ref, *outs
):
    first_ref, second_ref, whole_ref = outs
    rows, width = tok_ref.shape
    half = width // 2
    experts = 32
    row = lax.broadcasted_iota(jnp.int32, (rows, rows), 0)
    column = lax.broadcasted_iota(jnp.int32, (rows, rows), 1)
    upto = jnp.where(row <= column, 1.0, 0.0).astype(jnp.bfloat16)
    numbers = lax.broadcasted_iota(jnp.int32, (experts, rows), 0)
    gain = gain_ref[...].astype(jnp.float32)[None, :]
    own = (tok_ref, routes_ref, gates_ref)
    twin = (twin_ref, twin_routes_ref, twin_gates_ref)
    for c, (tokens, routes, gates) in enumerate((own, twin)):
        at = c * rows
        normed = scaled_rows(tokens[...], gain)
        if c == 0:
            whole_ref[...] = normed
        first_ref[at : at + rows, :half] = normed[:, :half]
        second_ref[at : at + rows, :] = normed[:, half:]
        chosen = jnp.zeros((experts, rows), jnp.float32)
        weight = jnp.zeros((experts, rows), jnp.float32)
        for k in range(routes.shape[0]):
            hit = routes[k : k + 1, :] == numbers
            chosen = jnp.where(hit, 1.0, chosen)
            weight = jnp.where(hit, gates[k : k + 1, :].astype(jnp.float32), weight)
        count = jnp.dot(chosen.astype(jnp.bfloat16), upto, preferred_element_type=jnp.float32)
        place = jnp.where(chosen > 0.5, count - 1.0, -1.0)
        first_ref[at : at + experts, half:] = place.astype(jnp.bfloat16)
        first_ref[at + experts : at + 2 * experts, half:] = weight.astype(jnp.bfloat16)
        first_ref[at + 2 * experts : at + rows, half:] = jnp.zeros(
            (rows - 2 * experts, rows), jnp.bfloat16
        )


def prepare(tokens, twin, norm_gain, routes, twin_routes, gates, twin_gates):
    rows, width = tokens.shape
    half = width // 2
    return pl.pallas_call(
        prep_kernel,
        out_shape=(
            jax.ShapeDtypeStruct((2 * rows, half + rows), jnp.bfloat16),
            jax.ShapeDtypeStruct((2 * rows, half), jnp.bfloat16),
            jax.ShapeDtypeStruct((rows, width), jnp.bfloat16),
        ),
        name="prepare",
    )(tokens, twin, norm_gain, routes, twin_routes, gates, twin_gates)


def across_columns(left, right):
    return lax.dot_general(left, right, (((1,), (1,)), ((), ())), preferred_element_type=jnp.float32)


def experts_kernel(ahead, chips, count, position_ref, last_ref, slots_ref, peer_last_ref, *refs):
    arrivals = 2 * chips - 1
    shared_hbm, peers_hbm, refs = refs[:5], refs[5 : 6 + count], refs[6 + count :]
    left_hbm, right_hbm, refs = refs[:arrivals], refs[arrivals : 2 * arrivals], refs[2 * arrivals :]
    gate_hbm, up_hbm, down_hbm, refs = *refs[:3], refs[3:]
    left_out, right_out, last_out = refs[:chips], refs[chips : 2 * chips], refs[2 * chips]
    parts_hbm, refs = refs[2 * chips + 1 : 2 * chips + 2 + count], refs[2 * chips + 2 + count :]
    left, right, gates, ups, downs, held, mix, incoming, outs, result = refs[:10]
    left_sem, right_sem, gate_sem, up_sem, down_sem, left_out_sem, right_out_sem = refs[10:17]
    shared_sem, peer_sem, part_sem = refs[17:]
    experts, width, hidden = gate_hbm.shape
    rows = left.shape[1] // 2
    half = width // 2
    numbered = held.shape[0]
    first = position_ref[0] * experts

    def load(hbm, buffer, sem, e):
        return pltpu.make_async_copy(hbm.at[e], buffer.at[e % 2], sem.at[e % 2])

    sides = ((left_hbm, left, left_sem), (right_hbm, right, right_sem))

    def fetch(side, d):
        hbm, buffer, sem = side
        return pltpu.make_async_copy(hbm[d], buffer.at[d], sem.at[d])

    def fetch_swapped(side, d):
        hbm, buffer, sem = side
        for c in range(2):
            pltpu.make_async_copy(
                hbm[arrivals - d].at[pl.ds((1 - c) * rows, rows)],
                buffer.at[d, pl.ds(c * rows, rows)],
                sem.at[d],
            ).start()

    chip, core = lax.div(position_ref[0], 2), lax.rem(position_ref[0], 2)
    for d in range(chips):
        near = (core == 0) & (chip >= d) | (core == 1) & (chip + d < chips)
        for side in sides:
            if d == 0:
                fetch(side, d).start()
            else:
                pl.when(near)(lambda: fetch(side, d).start())
                pl.when(jnp.logical_not(near))(lambda: fetch_swapped(side, d))
    gate_in = [load(gate_hbm, gates, gate_sem, e) for e in range(experts)]
    up_in = [load(up_hbm, ups, up_sem, e) for e in range(experts)]
    down_in = [load(down_hbm, downs, down_sem, e) for e in range(experts)]
    order = [copy for e in range(experts) for copy in (gate_in[e], up_in[e], down_in[e])]
    for copy in order[:ahead]:
        copy.start()

    def arrived(i):
        order[i].wait()
        if i + ahead < len(order):
            order[i + ahead].start()

    per = incoming.shape[1] // rows
    peer_in = []
    for p in range(count + 1):
        q = min(p, count - 1)
        to = incoming.at[q // per, pl.ds(q % per * rows, rows)]
        if p >= count - 1:
            to = to.at[:, pl.ds((p - count + 1) * half, half)]
        peer_in.append(pltpu.make_async_copy(peers_hbm[p], to, peer_sem.at[p]))
    begins = [0]
    for hbm in shared_hbm:
        begins.append(begins[-1] + hbm.shape[0])
    shared_in = [
        pltpu.make_async_copy(
            hbm, downs.at[0, pl.ds(begin, hbm.shape[0])], shared_sem.at[i]
        )
        for i, (hbm, begin) in enumerate(zip(shared_hbm, begins))
    ]
    slots = lax.broadcasted_iota(jnp.int32, (CAP, rows), 0).astype(jnp.float32)
    for d in range(chips):
        for side in sides:
            fetch(side, d).wait()
        for c in range(2):
            s = 2 * d + c
            own = pl.ds(c * rows, rows)
            held[...] = left[d, pl.ds(c * rows, numbered), half:].astype(jnp.float32)
            picks = []
            for e in range(experts):
                place = held[pl.ds(first + e, 1), :]
                weight = held[pl.ds(first + numbered // 2 + e, 1), :]
                hit = place == slots
                picks.append(jnp.where(hit, 1.0, 0.0))
                mix[s, e * CAP : (e + 1) * CAP, :] = jnp.where(hit, weight, 0.0).astype(
                    jnp.bfloat16
                )
            pick = jnp.concatenate(picks, axis=0).astype(jnp.bfloat16)
            for ref, to in ((left, 0), (right, half)):
                chosen = jnp.dot(pick, ref[d, own, :half], preferred_element_type=jnp.float32)
                chosen = chosen.astype(jnp.bfloat16)
                for e in range(experts):
                    incoming[e, s * CAP : (s + 1) * CAP, to : to + half] = chosen[
                        e * CAP : (e + 1) * CAP
                    ]
    for e in range(experts):
        inputs = incoming[e]
        arrived(3 * e)
        gate = jnp.dot(inputs, gates[e % 2], preferred_element_type=jnp.float32)
        arrived(3 * e + 1)
        up = jnp.dot(inputs, ups[e % 2], preferred_element_type=jnp.float32)
        mid = (gate / (1.0 + jnp.exp(-gate)) * up).astype(jnp.bfloat16)
        arrived(3 * e + 2)
        out = jnp.dot(mid, downs[e % 2], preferred_element_type=jnp.float32).astype(jnp.bfloat16)
        for s in range(2 * chips):
            outs[s, e * CAP : (e + 1) * CAP, :] = out[s * CAP : (s + 1) * CAP]
        if e == experts - 2:
            for copy in peer_in + shared_in:
                copy.start()
    sent = []
    for d in range(chips):
        for c in range(2):
            result[d, c * rows : (c + 1) * rows, :] = lax.dot_general(
                mix[2 * d + c],
                outs[2 * d + c],
                (((0,), (0,)), ((), ())),
                preferred_element_type=jnp.float32,
            ).astype(jnp.bfloat16)
        sent.append(
            pltpu.make_async_copy(result.at[d, :, :half], left_out[d], left_out_sem.at[d])
        )
        sent.append(
            pltpu.make_async_copy(result.at[d, :, half:], right_out[d], right_out_sem.at[d])
        )
        sent[-2].start()
        sent[-1].start()
    for copy in peer_in + shared_in:
        copy.wait()
    gate_ref, up_ref, down_ref, lower_ref, upper_ref = [
        downs.at[0, pl.ds(begin, hbm.shape[0])] for hbm, begin in zip(shared_hbm, begins)
    ]
    batch = incoming.shape[1]
    at = lax.broadcasted_iota(jnp.int32, (last_ref.shape[0], batch), 1)
    last = None
    inputs = incoming[: count // per].reshape(count * rows, width)
    gate = across_columns(inputs, gate_ref[...])
    up = across_columns(inputs, up_ref[...])
    mids = (gate / (1.0 + jnp.exp(-gate)) * up).astype(jnp.bfloat16)
    lows = across_columns(inputs, lower_ref[...])
    place = lax.broadcasted_iota(jnp.int32, lows.shape, 1) - slots_ref[...] * RANK
    lows = jnp.where((place >= 0) & (place < RANK), lows, 0.0).astype(jnp.bfloat16)
    for b in range(count // per):
        mid = mids[b * batch : (b + 1) * batch]
        low = lows[b * batch : (b + 1) * batch]
        part = jnp.dot(mid, down_ref[...], preferred_element_type=jnp.float32)
        part = part + jnp.dot(low, upper_ref[...], preferred_element_type=jnp.float32)
        part = part.astype(jnp.bfloat16)
        store = experts - count // per + b
        incoming[store] = part
        for c in range(per):
            p = per * b + c
            value = incoming.at[store, pl.ds(c * rows, rows)]
            values = [value]
            if p == count - 1:
                values = [value.at[:, pl.ds(0, half)], value.at[:, pl.ds(half, half)]]
            for i, value in enumerate(values):
                sent.append(pltpu.make_async_copy(value, parts_hbm[p + i], part_sem.at[p + i]))
                sent[-1].start()
        pick = jnp.where(peer_last_ref[...] - b * batch == at, 1.0, 0.0).astype(jnp.bfloat16)
        term = jnp.dot(pick, part, preferred_element_type=jnp.float32)
        last = term if last is None else last + term
    at = lax.broadcasted_iota(jnp.int32, (last_ref.shape[0], 2 * rows), 1)
    for d in range(chips):
        pick = jnp.where(last_ref[...] - d * 2 * rows == at, 1.0, 0.0).astype(jnp.bfloat16)
        last = last + jnp.dot(pick, result[d], preferred_element_type=jnp.float32)
    last_out[...] = last[: last_out.shape[0]]
    for copy in sent:
        copy.wait()


def run_experts(
    position, last_at, slots_at, peer_last, shared, peers, left, right, gate, up, down, requests
):
    experts, width, hidden = gate.shape
    arrivals = len(left)
    count = len(peers) - 1
    chips = (arrivals + 1) // 2
    both = left[0].shape[0]
    rows = both // 2
    half = width // 2
    slots = 2 * chips * CAP
    anywhere = pl.BlockSpec(memory_space=pltpu.MemorySpace.HBM)
    inside = pl.BlockSpec(memory_space=pltpu.VMEM)
    passed = jax.ShapeDtypeStruct((both, half), jnp.bfloat16)
    return pl.pallas_call(
        functools.partial(experts_kernel, AHEAD, chips, count),
        in_specs=[pl.BlockSpec(memory_space=pltpu.SMEM)]
        + [inside] * 3
        + [anywhere] * (6 + count + 2 * arrivals + 3),
        out_specs=[anywhere] * (2 * chips) + [inside] + [anywhere] * (count + 1),
        out_shape=[passed] * (2 * chips)
        + [jax.ShapeDtypeStruct((requests, width), jnp.float32)]
        + [jax.ShapeDtypeStruct((rows, width), jnp.bfloat16)] * (count - 1)
        + [jax.ShapeDtypeStruct((rows, half), jnp.bfloat16)] * 2,
        scratch_shapes=[
            pltpu.VMEM((chips, both, half + rows), jnp.bfloat16),
            pltpu.VMEM((chips, both, half), jnp.bfloat16),
            pltpu.VMEM((2, width, hidden), jnp.bfloat16),
            pltpu.VMEM((2, width, hidden), jnp.bfloat16),
            pltpu.VMEM((2, hidden, width), jnp.bfloat16),
            pltpu.VMEM((64, rows), jnp.float32),
            pltpu.VMEM((2 * chips, experts * CAP, rows), jnp.bfloat16),
            pltpu.VMEM((experts, slots, width), jnp.bfloat16),
            pltpu.VMEM((2 * chips, experts * CAP, width), jnp.bfloat16),
            pltpu.VMEM((chips, both, width), jnp.bfloat16),
            pltpu.SemaphoreType.DMA((chips,)),
            pltpu.SemaphoreType.DMA((chips,)),
            pltpu.SemaphoreType.DMA((2,)),
            pltpu.SemaphoreType.DMA((2,)),
            pltpu.SemaphoreType.DMA((2,)),
            pltpu.SemaphoreType.DMA((chips,)),
            pltpu.SemaphoreType.DMA((chips,)),
            pltpu.SemaphoreType.DMA((5,)),
            pltpu.SemaphoreType.DMA((count + 1,)),
            pltpu.SemaphoreType.DMA((count + 1,)),
        ],
        compiler_params=pltpu.CompilerParams(vmem_limit_bytes=60 << 20),
        cost_estimate=pl.CostEstimate(
            flops=6 * experts * slots * width * hidden,
            bytes_accessed=6 * experts * width * hidden,
            transcendentals=experts * slots * hidden,
        ),
        name="run_experts",
    )(position, last_at, slots_at, peer_last, *shared, *peers, *left, *right, gate, up, down)


def add(*terms):
    total = terms[0].astype(jnp.float32)
    for term in terms[1:]:
        total = total + term.astype(jnp.float32)
    return total.astype(jnp.bfloat16)


def swapped(value):
    rows = value.shape[0] // 2
    return jnp.concatenate([value[rows:], value[:rows]])


def twin_of(value, tensor_size):
    return lax.ppermute(value, "tensor", [(i, i ^ 1) for i in range(tensor_size)])


def along(value, chips, distance, begin=0, end=None):
    end = chips - distance if end is None else end
    upward = [(2 * z, 2 * (z + distance)) for z in range(begin, end)]
    downward = [
        (2 * (chips - 1 - z) + 1, 2 * (chips - 1 - z - distance) + 1) for z in range(begin, end)
    ]
    return lax.ppermute(value, "tensor", upward + downward)


def spread(chunks, chips):
    groups = [[chunk] for chunk in chunks]
    for k in range(1, chips):
        for group in groups:
            group.append(along(group[-1], chips, 1, k - 1))
    return groups


def collect(parts, chips, begin):
    run = [None] * len(parts)
    rows = parts[0][0].shape[0]
    for k in range(1, chips):
        for j, part in enumerate(parts):
            got = swapped(twin_of(part[chips - k], 2 * chips))
            terms = (part[k], got) if run[j] is None else (part[k], got, run[j][:rows])
            sent = add(*terms)
            if k == 1 and j == 0:
                carried, came = begin(sent)
                carry = carried
            if k == chips - 1 and j == len(parts) - 1:
                sent, *came = lax.optimization_barrier((sent, *came))
            if j == len(parts) - 1:
                if k > 1:
                    carry = add(carried, run[j][rows:])
                sent = jnp.concatenate([sent, carry])
            run[j] = along(sent, chips, 1, 0, k)
    done = []
    for j, part in enumerate(parts):
        total = add(part[0], run[j][:rows])
        own, other = total[: rows // 2], total[rows // 2 :]
        if j == len(parts) - 1:
            other = jnp.concatenate([other, run[j][rows:]])
        got = twin_of(other, 2 * chips)
        done.append((own, got[: rows // 2]))
    return done, came, [carried, run[-1][rows:], got[rows // 2 :]]


def across(value, combine, axis, size):
    step = 1
    while step < size:
        pairs = [(i, i ^ step) for i in range(lax.axis_size(axis))]
        value = combine(value, lax.ppermute(value, axis, pairs))
        step *= 2
    return value


def sent_along(value, axis, steps, size):
    return [lax.ppermute(value, axis, [(i, i ^ step) for i in range(size)]) for step in steps]


def after(values, other):
    *values, _ = lax.optimization_barrier((*values, other))
    return values


def summed(values):
    result = values[0].astype(jnp.float32)
    for value in values[1:]:
        result = result + value.astype(jnp.float32)
    return result


def from_peer(value, step, size):
    return lax.ppermute(value, "dp", [(i, i ^ step) for i in range(size)])


def local_line(
    tokens,
    norm_gain,
    routes,
    route_gates,
    lengths,
    request_adapter,
    adapter_slot,
    expert_gate,
    expert_up,
    expert_down,
    shared_gate,
    shared_up_weight,
    shared_down,
    adapter_down,
    adapter_up,
    head_weight,
):
    tok_rows, width = tokens.shape
    tensor_size = lax.axis_size("tensor")
    data_size = lax.axis_size("dp")
    tensor_pos = lax.axis_index("tensor")
    data_pos = lax.axis_index("dp")
    chips = tensor_size // 2
    small = (routes.T, route_gates.T)
    own = (tokens, *small)
    twin = [twin_of(value, tensor_size) for value in own]
    first, second, normed = prepare(
        tokens, twin[0], norm_gain, small[0], twin[1], small[1], twin[2]
    )
    left, right = spread([first, second], chips)
    near = [from_peer(normed, d, data_size) for d in (1, 2)]
    peers = [
        normed,
        *near,
        from_peer(near[1][:, : width // 2], 1, data_size),
        from_peer(near[0][:, width // 2 :], 2, data_size),
    ]
    block_rows = jnp.arange(tok_rows, dtype=jnp.int32)
    peer_dp = jnp.arange(data_size, dtype=jnp.int32) ^ data_pos
    bases = (peer_dp * tensor_size + tensor_pos) * tok_rows
    peer_positions = (bases[:, None] + block_rows[None, :]).reshape(-1)
    peer_slots = token_slots(peer_positions, lengths, request_adapter, adapter_slot)
    held_count, _, rank = adapter_down.shape
    held_slots = (peer_slots - data_pos * held_count)[:, None]
    lower = jnp.transpose(adapter_down, (0, 2, 1)).reshape(held_count * rank, width)
    upper = adapter_up.reshape(held_count * rank, width)
    ends = jnp.cumsum(lengths) - 1
    owner, row = ends // tok_rows, ends % tok_rows
    owner_dp, owner_tensor = owner // tensor_size, owner % tensor_size
    requests = ends.shape[0]
    chip, core = tensor_pos // 2, tensor_pos % 2
    steps = jnp.where(core == 0, chip - owner_tensor // 2, owner_tensor // 2 - chip) % chips
    away = (2 * steps + (owner_tensor % 2 != core)) * tok_rows + row
    line_at = jnp.where(owner_dp == data_pos, away, -1)
    across_at = (owner_dp ^ data_pos) * tok_rows + row
    peer_at = jnp.where(owner_tensor == tensor_pos, across_at, -1)
    padding = ((0, -requests % 16), (0, 0))
    line_at = jnp.pad(line_at[:, None], padding, constant_values=-1)
    peer_at = jnp.pad(peer_at[:, None], padding, constant_values=-1)
    early = after(left[1:-1] + right[1:-1], right[-2])
    early = [early[: chips - 2], early[chips - 2 :]]
    left = left + [twin_of(part, tensor_size) for part in early[0] + left[-1:]]
    right = right + [twin_of(part, tensor_size) for part in early[1] + right[-1:]]
    results = run_experts(
        tensor_pos.astype(jnp.int32).reshape(1),
        line_at,
        held_slots,
        peer_at,
        [shared_gate.T, shared_up_weight.T, shared_down, lower, upper],
        peers,
        left,
        right,
        expert_gate,
        expert_up,
        expert_down,
        requests,
    )
    passed, last, parts = results[: 2 * chips], results[2 * chips], results[2 * chips + 1 :]
    half = width // 2

    def begin(ready):
        value, *tied = after([last, *parts], ready)
        value = across(value, jnp.add, "tensor", 2)
        sent = value.astype(jnp.bfloat16)
        value = summed([value] + sent_along(sent, "dp", range(1, data_size), data_size))
        far = [from_peer(tied[3], 1, data_size), from_peer(tied[4], 2, data_size)]
        joined = [
            jnp.concatenate([tied[1][:, :half], add(tied[1][:, half:], far[1])], axis=1),
            jnp.concatenate([add(tied[2][:, :half], far[0]), tied[2][:, half:]], axis=1),
        ]
        came = [from_peer(joined[0], 1, data_size), from_peer(joined[1], 2, data_size)]
        value = value.astype(jnp.bfloat16)
        return jnp.concatenate([value[:, :half], value[:, half:]]), came

    routed, came, carried = collect([passed[:chips], passed[chips:]], chips, begin)
    last = summed(carried)
    last = jnp.concatenate([last[:requests], last[requests:]], axis=1).astype(jnp.bfloat16)
    last_values = last.astype(jnp.float32)
    last_norm = jnp.sqrt(jnp.sum(last_values * last_values, axis=1))
    logits = jnp.dot(last, head_weight, preferred_element_type=jnp.float32)
    top = jnp.max(logits, axis=1, keepdims=True)
    tops = [top] + sent_along(top, "dp", range(1, data_size), data_size)
    block_logit = functools.reduce(jnp.maximum, tops)
    out = jnp.concatenate([a.astype(jnp.float32) + b.astype(jnp.float32) for a, b in routed], axis=1)
    out = out + summed([parts[0], *came])
    return (out.astype(jnp.bfloat16), last_norm, block_logit)


def solution(mesh):
    placed = (
        P(("dp", "tensor"), None),
        P(),
        P(("dp", "tensor"), None),
        P(("dp", "tensor"), None),
        P(),
        P(),
        P(),
        P("tensor", None, None),
        P("tensor", None, None),
        P("tensor", None, None),
        P(None, "dp"),
        P(None, "dp"),
        P("dp", None),
        P("dp", None, None),
        P("dp", None, None),
        P(None, ("dp", "tensor")),
    )
    short = mesh.shape["tensor"] == 8 and mesh.shape["dp"] == 4
    return jax.shard_map(
        local_line if short else local,
        mesh=mesh,
        in_specs=placed,
        out_specs=(P(("dp", "tensor"), None), P(), P(None, "tensor")),
        check_vma=False,
    )
```
